256 devices in a mesh: tm: 4 (over x), sx: 16 (over z, core), sy: 4 (over y).
Axes of the slice: x: 4, y: 4, z: 8, core: 2. Of those that a mesh axis runs over, the one named last changes fastest.
Arguments:
- initial_state: float32 [4, 256, 64, 128], P(None, 'sx', 'sy'), may hold values from -6 to 6
- start_old: float32 [4, 4, 256, 64, 128], P('tm', None, 'sx', 'sy'), may hold values from -6 to 6
- end_old: float32 [4, 4, 256, 64, 128], P('tm', None, 'sx', 'sy'), may hold values from -6 to 6
- coarse_old: float32 [4, 4, 128, 32, 64], P('tm', None, 'sx', 'sy'), may hold values from -6 to 6
Outputs:
- new_start: float32 [4, 4, 256, 64, 128], P('tm', None, 'sx', 'sy')
- fine_end: float32 [4, 4, 256, 64, 128], P('tm', None, 'sx', 'sy')
- coarse_end: float32 [4, 4, 128, 32, 64], P('tm', None, 'sx', 'sy')
The draws below stay inside these ranges and needn't reach their ends.
All inputs are finite; a program needn't handle non-finite values.
Results may differ from the reference program's by a relative error of at most 0.0001.
Values sent between devices are 32-bit elements; how exact they have to be, the bound alone decides.
No kernel may reach another device: no remote copies, remote signals or barrier semaphores. Data moves between devices by JAX's collectives and lax.ppermute only.
A program may use at most 128 MiB of HBM per device.

```python
import jax
import jax.numpy as jnp

LEVELS = 5
SWEEPS = 3
SLICES = 4
NX = 256
NY = 64
NZ = 128


def block_scale(own_key, shape, cuts, least, largest):
    def one(position, shards_of):
        draws = jax.random.uniform(jax.random.fold_in(jax.random.fold_in(own_key, 6), position), (shards_of,), jnp.float32, least / len(cuts), largest / len(cuts))
        return jnp.repeat(jnp.exp(draws), shape[position] // shards_of).reshape((-1,) + (1,) * (len(shape) - position - 1))

    gain = one(*cuts[0])
    for cut in cuts[1:]:
        gain = gain * one(*cut)
    return gain


def scatter_about(stream_key, dims, deviation, most, pieces=(), held_as=jnp.bfloat16):
    drawn = jax.random.normal(stream_key, dims, jnp.float32) * deviation
    if len(pieces) > 0:
        drawn = block_scale(stream_key, dims, pieces, -0.22, 0.18) * drawn
    return jnp.clip(drawn, min=-most, max=most).astype(held_as)


def setup_inputs(seed: int = 0) -> dict:
    splits = jax.random.split(jax.random.key(seed), 5)
    initial_state = scatter_about(splits[0], (4, NX, NY, NZ), 1.0, 6.0, ((1, 16), (2, 4)), jnp.float32)
    start_old = scatter_about(splits[1], (SLICES, 4, NX, NY, NZ), 1.0, 6.0, ((0, 4), (2, 16), (3, 4)), jnp.float32)
    end_old = scatter_about(splits[2], (SLICES, 4, NX, NY, NZ), 1.0, 6.0, ((0, 4), (2, 16), (3, 4)), jnp.float32)
    coarse_old = scatter_about(splits[3], (SLICES, 4, NX // 2, NY // 2, NZ // 2), 1.0, 6.0, ((0, 4), (2, 16), (3, 4)), jnp.float32)
    return dict(initial_state=initial_state, start_old=start_old, end_old=end_old, coarse_old=coarse_old)


OMEGA = 2.0 / 3.0
STEP = 0.5


def plus_x(padded):
    return padded[..., 2:, 1:-1, :]


def minus_x(padded):
    return padded[..., :-2, 1:-1, :]


def plus_y(padded):
    return padded[..., 1:-1, 2:, :]


def minus_y(padded):
    return padded[..., 1:-1, :-2, :]


def centre(padded):
    return padded[..., 1:-1, 1:-1, :]


def plus_z(field):
    return jnp.roll(field, -1, -1)


def minus_z(field):
    return jnp.roll(field, 1, -1)


def periodic_pad(field):
    widths = [(0, 0)] * (field.ndim - 3) + [(1, 1), (1, 1), (0, 0)]
    return jnp.pad(field, widths, mode="wrap")


def neighbours(padded):
    middle = centre(padded)
    return plus_x(padded) + minus_x(padded) + plus_y(padded) + minus_y(padded) + plus_z(middle) + minus_z(middle)


def relax_once(padded, source, spacing_sq):
    middle = centre(padded)
    return middle + OMEGA * ((neighbours(padded) - spacing_sq * source) / 6.0 - middle)


def first_relax(source, spacing_sq):
    return OMEGA * ((0.0 - spacing_sq * source) / 6.0)


def defect(padded, source, spacing_sq):
    return source - (neighbours(padded) - 6.0 * centre(padded)) / spacing_sq


def restrict(field):
    lead = field.shape[:-3]
    size_x, size_y, size_z = field.shape[-3:]
    blocks = field.reshape(lead + (size_x // 2, 2, size_y // 2, 2, size_z // 2, 2))
    return blocks.mean(axis=(-5, -3, -1))


def prolong(field):
    return jnp.repeat(jnp.repeat(jnp.repeat(field, 2, -3), 2, -2), 2, -1)


def explicit_rate(padded, per_cell):
    middle = centre(padded)
    grad_x = (plus_x(padded) - minus_x(padded)) * 0.5
    grad_y = (plus_y(padded) - minus_y(padded)) * 0.5
    grad_z = (plus_z(middle) - minus_z(middle)) * 0.5
    carried = -(middle[0] * grad_x + middle[1] * grad_y + middle[2] * grad_z) * per_cell
    lifted = jnp.concatenate([carried[:2], carried[2:3] + middle[3:4], carried[3:]], axis=0)
    return STEP * lifted


def divergence(pad_u, pad_v, middle_w, per_cell):
    total = (plus_x(pad_u) - minus_x(pad_u)) * 0.5 + (plus_y(pad_v) - minus_y(pad_v)) * 0.5
    total = total + (plus_z(middle_w) - minus_z(middle_w)) * 0.5
    return total * per_cell


def correct(combined, padded, per_cell):
    middle = centre(padded)
    grad_x = (plus_x(padded) - minus_x(padded)) * 0.5 * per_cell
    grad_y = (plus_y(padded) - minus_y(padded)) * 0.5 * per_cell
    grad_z = (plus_z(middle) - minus_z(middle)) * 0.5 * per_cell
    return jnp.stack([combined[0] - grad_x, combined[1] - grad_y, combined[2] - grad_z, combined[3]])


def vcycle(source, level):
    spacing_sq = 4.0 ** level
    estimate = first_relax(source, spacing_sq)
    if level == LEVELS - 1:
        for counter in range(SWEEPS - 1):
            estimate = relax_once(periodic_pad(estimate), source, spacing_sq)
        return estimate
    coarser = vcycle(restrict(defect(periodic_pad(estimate), source, spacing_sq)), level + 1)
    estimate = estimate + prolong(coarser)
    return relax_once(periodic_pad(estimate), source, spacing_sq)


def project(combined, level):
    per_cell = 0.5 ** level
    source = divergence(periodic_pad(combined[0]), periodic_pad(combined[1]), combined[2], per_cell)
    pressure = vcycle(source, level)
    return correct(combined, periodic_pad(pressure), per_cell)


def reference(initial_state, start_old, end_old, coarse_old):
    fine_list = []
    for slice_id in range(SLICES):
        begin_state = start_old[slice_id]
        end_state = end_old[slice_id]
        combined = begin_state + 0.5 * (explicit_rate(periodic_pad(begin_state), 1.0) + explicit_rate(periodic_pad(end_state), 1.0))
        fine_list.append(project(combined, 0))
    current = restrict(initial_state)
    starts = [initial_state]
    coarse_list = []
    for slice_id in range(SLICES):
        combined = current + explicit_rate(periodic_pad(current), 0.5)
        coarse_out = project(combined, 1)
        coarse_list.append(coarse_out)
        jump_fine = fine_list[slice_id] - prolong(coarse_old[slice_id])
        current = coarse_out + restrict(jump_fine)
        starts.append(jump_fine + prolong(coarse_out))
    return jnp.stack(starts[:SLICES]), jnp.stack(fine_list), jnp.stack(coarse_list)
```

```python
import jax
import jax.numpy as jnp
from jax import lax
from jax.experimental import pallas as pl
from jax.experimental.pallas import tpu as pltpu
from jax.sharding import PartitionSpec as P

F32 = jnp.float32
HIGH = lax.Precision.HIGHEST


def call(body, outs, args, scratch=(), smem=0, limit=24):
    vmem = pl.BlockSpec(memory_space=pltpu.VMEM)
    scalar = pl.BlockSpec(memory_space=pltpu.SMEM)
    single = not isinstance(outs, list)
    shapes = [outs] if single else outs
    got = pl.pallas_call(
        body,
        out_shape=[jax.ShapeDtypeStruct(s, F32) for s in shapes],
        in_specs=[scalar] * smem + [vmem] * (len(args) - smem),
        out_specs=[vmem] * len(shapes),
        scratch_shapes=[pltpu.VMEM(s, F32) for s in scratch],
        compiler_params=pltpu.CompilerParams(vmem_limit_bytes=limit * 2**20),
        name=body.__name__,
    )(*args)
    return got[0] if single else got


def shifted(value, amount, axis):
    return pltpu.roll(value, amount % value.shape[axis], axis)


def nxt(value, step, axis):
    return shifted(value, -step, axis)


def prv(value, step, axis):
    return shifted(value, step, axis)


def index_along(shape, axis):
    return lax.broadcasted_iota(jnp.int32, shape, axis)


def pair_sum(value, step, axis):
    upper = (index_along(value.shape, axis) // step) % 2 == 1
    return value + jnp.where(upper, prv(value, step, axis), nxt(value, step, axis))


def ring_sum(value, step_y, step_z):
    return (
        nxt(value, step_y, 0)
        + prv(value, step_y, 0)
        + nxt(value, step_z, 1)
        + prv(value, step_z, 1)
    )


def restricted_defect(before, first, second, after, step_y, step_z):
    both = first + second
    total = both * (1.0 / 3.0) + (before + both + after + ring_sum(both, step_y, step_z)) * (1.0 / 9.0)
    return pair_sum(pair_sum(total, step_y, 0), step_z, 1) * 0.125


def smoothed(before, here, after, source, spacing_sq, step_y, step_z):
    around = before + after + ring_sum(here, step_y, step_z)
    return here * (1.0 / 3.0) + (around - spacing_sq * source) * (1.0 / 9.0)


def deep_pressure(r3, step_y, step_z):
    r4 = [
        restricted_defect(r3[2 * w], r3[2 * w + 1], r3[2 * w + 2], r3[2 * w + 3], step_y, step_z)
        for w in range(7)
    ]
    low_y, low_z = 2 * step_y, 2 * step_z
    p4 = [r * (-256.0 / 9.0) for r in r4]
    for sweep in range(2):
        inner = range(1 + sweep, 6 - sweep)
        fresh = {w: smoothed(p4[w - 1], p4[w], p4[w + 1], r4[w], 256.0, low_y, low_z) for w in inner}
        p4 = [fresh.get(w) for w in range(7)]
    e3 = {q: r3[q] * (-64.0 / 9.0) + p4[(q - 7) // 2 + 3] for q in range(5, 11)}
    return [
        smoothed(e3[q - 1], e3[q], e3[q + 1], r3[q], 64.0, step_y, step_z) for q in range(6, 10)
    ]


def advected(ref, base, i, comp):
    here = ref[base + comp, i]
    grad_x = ref[base + comp, i + 1] - ref[base + comp, i - 1]
    grad_y = nxt(here, 1, 0) - prv(here, 1, 0)
    grad_z = nxt(here, 1, 1) - prv(here, 1, 1)
    return ref[base, i] * grad_x + ref[base + 1, i] * grad_y + ref[base + 2, i] * grad_z


def z_pick(high):
    k = index_along((128, 128), 0)
    j = index_along((128, 128), 1)
    return jnp.where(k // 2 == j - 64 * high, 1.0, 0.0).astype(F32)


def z_spread(high):
    k = index_along((128, 128), 0)
    j = index_along((128, 128), 1)
    return jnp.where(k == j // 2 + 64 * high, 1.0, 0.0).astype(F32)


def dot(a, b):
    return lax.dot_general(a, b, (((1,), (0,)), ((), ())), precision=HIGH, preferred_element_type=F32)


def restricted_packed(fine, rows, half):
    for comp in range(4):
        for big in range(8):
            rows[comp, big] = fine[comp, 2 * big] + fine[comp, 2 * big + 1]
    for comp in range(4):
        for big in range(8):
            half[comp, big] = rows[comp, big, pl.ds(0, 8, 2), :] + rows[comp, big, pl.ds(1, 8, 2), :]
    low, high = z_pick(0), z_pick(1)
    return [
        0.125
        * (
            dot(half[2 * h].reshape(64, 128), low)
            + dot(half[2 * h + 1].reshape(64, 128), high)
        )
        for h in range(2)
    ]


def opening_body(initial, out, rows, half):
    packed = restricted_packed(initial, rows, half)
    for h in range(2):
        out[h] = packed[h].reshape(8, 8, 128)


def fine_source_body(begin, end, left, right, low, high, comb_out, r0_out, state, comb):
    for f in range(8):
        own = begin if f < 4 else end
        c = f % 4
        state[f, 0:2, 4:20] = left[f]
        state[f, 2:18, 4:20] = own[c]
        state[f, 18:20, 4:20] = right[f]
        state[f, :, 2:4] = low[f]
        state[f, :, 20:22] = high[f]

    def one(i, carry):
        for c in range(4):
            total = state[c, i] - 0.125 * (advected(state, 0, i, c) + advected(state, 4, i, c))
            if c == 2:
                total = total + 0.25 * (state[3, i] + state[7, i])
            comb[c, i - 1] = total
        return carry

    lax.fori_loop(1, 19, one, 0)

    def two(x, carry):
        v = comb[1, x + 1]
        w = comb[2, x + 1]
        div = comb[0, x + 2] - comb[0, x] + nxt(v, 1, 0) - prv(v, 1, 0) + nxt(w, 1, 1) - prv(w, 1, 1)
        r0_out[x] = (0.5 * div)[4:20]
        for c in range(4):
            comb_out[c, x] = comb[c, x + 1, 4:20, :]
        return carry

    lax.fori_loop(0, 16, two, 0)


def fine_down_body(own, left, right, low, high, r0, r1, r2p):
    r0[0:5, 8:24] = left[...]
    r0[5:21, 8:24] = own[...]
    r0[21:26, 8:24] = right[...]
    r0[:, 0:8] = low[...]
    r0[:, 24:32] = high[...]

    def one(k, carry):
        a = 2 * k + 1
        r1[k] = restricted_defect(r0[a - 1], r0[a], r0[a + 1], r0[a + 2], 1, 1)
        return carry

    lax.fori_loop(0, 12, one, 0)
    row = index_along((32, 128), 0)
    lane = index_along((32, 128), 1)
    mine = (row >= 8) & (row < 24) & (row % 4 == 0) & (lane % 4 == row // 4 - 2)
    for m in range(4):
        k = 2 * m + 2
        r2 = restricted_defect(r1[k - 1], r1[k], r1[k + 1], r1[k + 2], 2, 2)
        r2p[m : m + 1, :] = jnp.sum(jnp.where(mine, r2, 0.0), axis=0, keepdims=True)


def fine_up_body(where, gathered, r1, r0, comb, old, fine, rj, r2, e2, p2, e1, p1, e0, p0, rows, half):
    sx, sy = where[0], where[1]
    for d in range(9):
        for b in range(4):
            peer = ((sx + d + 12) % 16) * 4 + (sy + b + 3) % 4
            block = gathered[peer]
            for n in range(4):
                r2[4 * d + n, 4 * b : 4 * b + 4, :] = jnp.broadcast_to(block[n : n + 1], (4, 128))
    lane = index_along((16, 128), 1)
    row = index_along((16, 128), 0)
    mine = lane % 4 == row % 4

    def unpack(n, carry):
        r2[n] = pair_sum(pair_sum(jnp.where(mine, r2[n], 0.0), 1, 1), 2, 1)
        return carry

    lax.fori_loop(1, 35, unpack, 0)
    r3 = [
        restricted_defect(r2[2 * q + 1], r2[2 * q + 2], r2[2 * q + 3], r2[2 * q + 4], 1, 4)
        for q in range(16)
    ]
    p3 = deep_pressure(r3, 2, 8)
    for i in range(8):
        e2[i] = r2[14 + i] * (-16.0 / 9.0) + p3[i // 2]
    for i in range(6):
        value = smoothed(e2[i], e2[i + 1], e2[i + 2], r2[15 + i], 16.0, 1, 4)
        for y2 in range(8):
            p2[i, 4 * y2 : 4 * y2 + 4, :] = jnp.broadcast_to(value[y2 + 2 : y2 + 3], (4, 128))

    def lift(k, carry):
        e1[k] = r1[k] * (-4.0 / 9.0) + p2[k // 2]
        return carry

    lax.fori_loop(0, 12, lift, 0)

    def relax1(k, carry):
        p1[k] = smoothed(e1[k], e1[k + 1], e1[k + 2], r1[k + 1], 4.0, 2, 2)
        return carry

    lax.fori_loop(0, 10, relax1, 0)

    def lift0(j, carry):
        e0[j] = r0[j + 3] * (-1.0 / 9.0) + p1[j // 2]
        return carry

    lax.fori_loop(0, 20, lift0, 0)

    def relax0(j, carry):
        p0[j] = smoothed(e0[j], e0[j + 1], e0[j + 2], r0[j + 4], 1.0, 1, 1)
        return carry

    lax.fori_loop(0, 18, relax0, 0)

    def slope(x, carry):
        here = p0[x + 1]
        fine[0, x] = comb[0, x] - 0.5 * (p0[x + 2] - p0[x])[8:24]
        fine[1, x] = comb[1, x] - 0.5 * (nxt(here, 1, 0) - prv(here, 1, 0))[8:24]
        fine[2, x] = comb[2, x] - 0.5 * (nxt(here, 1, 1) - prv(here, 1, 1))[8:24]
        fine[3, x] = comb[3, x]
        return carry

    lax.fori_loop(0, 16, slope, 0)
    packed = restricted_packed(fine, rows, half)
    for h in range(2):
        rj[h] = packed[h].reshape(8, 8, 128) - old[h]


def coarse_down_body(left, own, right, comb_out, r1_out, r2_out, r3p, state, comb, r1):
    lane = index_along((32, 128), 1)
    row = index_along((32, 128), 0)
    for side, ref in enumerate((left, own, right)):

        def unpack(x, carry, side=side, ref=ref):
            for h in range(2):
                pair = ref[h, x]
                other = shifted(pair, 64, 1)
                state[2 * h, 8 * side + x] = jnp.where(lane < 64, pair, other)
                state[2 * h + 1, 8 * side + x] = jnp.where(lane < 64, other, pair)
            return carry

        lax.fori_loop(0, 8, unpack, 0)

    def one(i, carry):
        for c in range(3):
            total = state[c, i] - 0.125 * advected(state, 0, i, c)
            if c == 2:
                total = total + 0.5 * state[3, i]
            comb[c, i - 2] = total
        return carry

    lax.fori_loop(2, 22, one, 0)

    def own_b(x, carry):
        comb_out[3, x] = state[3, x + 8] - 0.125 * advected(state, 0, x + 8, 3)
        for c in range(3):
            comb_out[c, x] = comb[c, x + 6]
        return carry

    lax.fori_loop(0, 8, own_b, 0)

    def two(k, carry):
        v = comb[1, k + 1]
        w = comb[2, k + 1]
        div = comb[0, k + 2] - comb[0, k] + nxt(v, 1, 0) - prv(v, 1, 0) + nxt(w, 1, 1) - prv(w, 1, 1)
        r1[k] = 0.25 * div
        return carry

    lax.fori_loop(0, 18, two, 0)

    def three(m, carry):
        a = 2 * m + 1
        r2_out[m] = restricted_defect(r1[a - 1], r1[a], r1[a + 1], r1[a + 2], 1, 1)
        return carry

    lax.fori_loop(0, 8, three, 0)
    r1_out[...] = r1[3:15]
    mine = (row % 4 == 0) & (lane % 4 + 4 * (lane // 64) == row // 4)
    for x3 in range(2):
        m = 2 * x3 + 2
        r3 = restricted_defect(r2_out[m - 1], r2_out[m], r2_out[m + 1], r2_out[m + 2], 2, 2)
        r3p[x3 : x3 + 1, :] = jnp.sum(jnp.where(mine, r3, 0.0), axis=0, keepdims=True)


def coarse_up_core(where, gathered, comb, r1, r2, p3, p2, e2, e1, p1, emit):
    sx = where[0]
    lane = index_along((8, 128), 1)
    row = index_along((8, 128), 0)
    mine = lane % 4 + 4 * (lane // 64) == row
    r3 = []
    for q in range(16):
        x3 = q - 7
        block = gathered[(sx + x3 // 2 + 16) % 16]
        value = jnp.where(mine, jnp.broadcast_to(block[x3 % 2 : x3 % 2 + 1], (8, 128)), 0.0)
        value = value + shifted(value, 64, 1)
        r3.append(pair_sum(pair_sum(value, 1, 1), 2, 1))
    for i, value in enumerate(deep_pressure(r3, 1, 4)):
        for y3 in range(8):
            p3[i, 4 * y3 : 4 * y3 + 4, :] = jnp.broadcast_to(value[y3 : y3 + 1], (4, 128))

    def lift2(m, carry):
        e2[m] = r2[m] * (-16.0 / 9.0) + p3[m // 2]
        return carry

    lax.fori_loop(0, 8, lift2, 0)

    def relax2(m, carry):
        p2[m] = smoothed(e2[m], e2[m + 1], e2[m + 2], r2[m + 1], 16.0, 2, 2)
        return carry

    lax.fori_loop(0, 6, relax2, 0)

    def lift1(k, carry):
        e1[k] = r1[k] * (-4.0 / 9.0) + p2[k // 2]
        return carry

    lax.fori_loop(0, 12, lift1, 0)

    def relax1(k, carry):
        p1[k] = smoothed(e1[k], e1[k + 1], e1[k + 2], r1[k + 1], 4.0, 1, 1)
        return carry

    lax.fori_loop(0, 10, relax1, 0)
    lane = index_along((32, 128), 1)

    def slope(x, carry):
        here = p1[x + 1]
        u = comb[0, x] - 0.25 * (p1[x + 2] - p1[x])
        v = comb[1, x] - 0.25 * (nxt(here, 1, 0) - prv(here, 1, 0))
        w = comb[2, x] - 0.25 * (nxt(here, 1, 1) - prv(here, 1, 1))
        emit(x, jnp.where(lane < 64, u, v), jnp.where(lane < 64, w, comb[3, x]))
        return carry

    lax.fori_loop(0, 8, slope, 0)


def coarse_up_body(where, gathered, comb, r1, r2, ended, *scratch):
    def emit(x, uv, wb):
        ended[0, x] = uv
        ended[1, x] = wb

    coarse_up_core(where, gathered, comb, r1, r2, *scratch, emit)


def coarse_up_next_body(where, gathered, comb, r1, r2, jump, ended, following, *scratch):
    def emit(x, uv, wb):
        ended[0, x] = uv
        ended[1, x] = wb
        following[0, x] = uv + jump[0, x]
        following[1, x] = wb + jump[1, x]

    coarse_up_core(where, gathered, comb, r1, r2, *scratch, emit)


UP_SCRATCH = [(4, 32, 128), (6, 32, 128), (8, 32, 128), (12, 32, 128), (10, 32, 128)]


def rows_of(where, step):
    return pl.ds(pl.multiple_of(8 * ((where[1] + 4 - step) % 4), 8), 8)


def join_body(where, a0, a1, a2, a3, out):
    for step, ref in enumerate((a0, a1, a2, a3)):
        rows = rows_of(where, step)
        for h in range(2):
            for x in range(8):
                out[h, x, rows, :] = ref[h, x]


def join_jumps_body(where, a0, a1, a2, a3, ended, first, second, third):
    for step, ref in enumerate((a0, a1, a2, a3)):
        rows = rows_of(where, step)
        for h in range(2):
            for x in range(8):
                first[h, x, rows, :] = ref[0, h, x] + ended[h, x, rows, :]
                second[h, x, rows, :] = ref[1, h, x]
                third[h, x, rows, :] = ref[2, h, x]


def new_start_body(where, fine, initial, c1, c2, c3, out, rows, half, tall):
    t = where[2]

    @pl.when(t == 0)
    def _():
        out[...] = initial[...]

    @pl.when(t > 0)
    def _():
        packed = restricted_packed(fine, rows, half)
        mine = rows_of(where, 0)
        for h in range(2):
            state = jnp.where(
                t == 1, c1[h, :, mine, :], jnp.where(t == 2, c2[h, :, mine, :], c3[h, :, mine, :])
            )
            change = state.reshape(64, 128) - packed[h]
            for side in range(2):
                comp = 2 * h + side
                wide = dot(change, z_spread(side)).reshape(8, 8, 128)
                for x in range(8):
                    tall[comp, x, pl.ds(0, 8, 2), :] = wide[x]
                    tall[comp, x, pl.ds(1, 8, 2), :] = wide[x]
        for comp in range(4):
            for x in range(16):
                out[comp, x] = fine[comp, x] + tall[comp, x // 2]


def coarse_end_body(where, e0, e1, e2, e3, out):
    t = where[2]
    mine = rows_of(where, 0)
    for h in range(2):
        low = jnp.where(t == 0, e0[h, :, mine, :], e1[h, :, mine, :])
        high = jnp.where(t == 2, e2[h, :, mine, :], e3[h, :, mine, :])
        value = jnp.where(t < 2, low, high)
        out[2 * h] = value[:, :, :64]
        out[2 * h + 1] = shifted(value, 64, 2)[:, :, :64]


def moved(value, axis, step):
    count = lax.axis_size(axis)
    return lax.ppermute(value, axis, [(i, (i + step) % count) for i in range(count)])


def both_sides(low_face, high_face, axis):
    return moved(high_face, axis, 1), moved(low_face, axis, -1)


def around(value, axis):
    return [moved(value, axis, step) for step in range(1, 4)]


def shards(initial_state, start_old, end_old, coarse_old):
    begin, end, old = start_old[0], end_old[0], coarse_old[0]
    sx, sy, t = lax.axis_index("sx"), lax.axis_index("sy"), lax.axis_index("tm")
    where = jnp.stack([sx, sy, t]).astype(jnp.int32)

    opening = call(opening_body, (2, 8, 8, 128), [initial_state], [(4, 8, 16, 128), (4, 8, 8, 128)])
    old_packed = jnp.stack(
        [jnp.concatenate([old[0], old[1]], axis=-1), jnp.concatenate([old[2], old[3]], axis=-1)]
    )

    def face(cut):
        return jnp.concatenate([begin[cut], end[cut]], axis=0)

    every = slice(None)
    left, right = both_sides(
        face((every, slice(0, 2))), face((every, slice(14, 16))), "sx"
    )

    def y_face(cut):
        inner = face((every, every, cut))
        return jnp.concatenate([left[:, :, cut], inner, right[:, :, cut]], axis=1)

    low, high = both_sides(y_face(slice(0, 2)), y_face(slice(14, 16)), "sy")
    comb, r0 = call(
        fine_source_body,
        [(4, 16, 16, 128), (16, 16, 128)],
        [begin, end, left, right, low, high],
        [(8, 20, 24, 128), (4, 18, 24, 128)],
    )

    c0 = call(join_body, (2, 8, 32, 128), [where, opening] + around(opening, "sy"), smem=1)

    def coarse_down(state):
        lo, hi = both_sides(state, state, "sx")
        return call(
            coarse_down_body,
            [(4, 8, 32, 128), (12, 32, 128), (8, 32, 128), (2, 128)],
            [lo, state, hi],
            [(4, 24, 32, 128), (3, 20, 32, 128), (18, 32, 128)],
        )

    comb0, first0, second0, third0 = coarse_down(c0)

    left, right = both_sides(r0[:5], r0[11:], "sx")

    def source_face(cut):
        return jnp.concatenate([left[:, cut], r0[:, cut], right[:, cut]], axis=0)

    low, high = both_sides(source_face(slice(0, 8)), source_face(slice(8, 16)), "sy")
    r0_wide, r1, r2p = call(
        fine_down_body,
        [(26, 32, 128), (12, 32, 128), (4, 128)],
        [r0, left, right, low, high],
    )

    message = jnp.concatenate([r2p, third0, jnp.zeros((2, 128), F32)], axis=0)
    gathered = lax.all_to_all(jnp.broadcast_to(message[None], (64, 8, 128)), ("sx", "sy"), 0, 0)
    fine_end, rj = call(
        fine_up_body,
        [(4, 16, 16, 128), (2, 8, 8, 128)],
        [where, gathered, r1, r0_wide, comb, old_packed],
        [
            (36, 16, 128),
            (8, 16, 128),
            (6, 32, 128),
            (12, 32, 128),
            (10, 32, 128),
            (20, 32, 128),
            (18, 32, 128),
            (4, 8, 16, 128),
            (4, 8, 8, 128),
        ],
        smem=1,
    )
    ended0 = call(
        coarse_up_body,
        (2, 8, 32, 128),
        [where, gathered[::4, 4:6], comb0, first0, second0],
        UP_SCRATCH,
        smem=1,
    )

    turned = [rj] + around(rj, "tm")

    def slice_of(s):
        back = (t - s) % 4
        return jnp.where(
            back < 2,
            jnp.where(back == 0, turned[0], turned[1]),
            jnp.where(back == 2, turned[2], turned[3]),
        )

    jumps = jnp.stack([slice_of(s) for s in range(3)])
    c1, jump1, jump2 = call(
        join_jumps_body,
        [(2, 8, 32, 128)] * 3,
        [where, jumps] + around(jumps, "sy") + [ended0],
        smem=1,
    )
    fine_before = moved(fine_end, "tm", 1)

    def coarse_step(state, jump):
        combined, level1, level2, message = coarse_down(state)
        got = lax.all_to_all(jnp.broadcast_to(message[None], (16, 2, 128)), "sx", 0, 0)
        args = [where, got, combined, level1, level2]
        if jump is None:
            return call(coarse_up_body, (2, 8, 32, 128), args, UP_SCRATCH, smem=1)
        return call(
            coarse_up_next_body, [(2, 8, 32, 128)] * 2, args + [jump], UP_SCRATCH, smem=1
        )

    ended1, c2 = coarse_step(c1, jump1)
    ended2, c3 = coarse_step(c2, jump2)
    new_start = call(
        new_start_body,
        (4, 16, 16, 128),
        [where, fine_before, initial_state, c1, c2, c3],
        [(4, 8, 16, 128), (4, 8, 8, 128), (4, 8, 16, 128)],
        smem=1,
    )
    ended3 = coarse_step(c3, None)
    coarse_end = call(coarse_end_body, (4, 8, 8, 64), [where, ended0, ended1, ended2, ended3], smem=1)
    return (new_start[None], fine_end[None], coarse_end[None])


def solution(mesh):
    in_specs = (
        P(None, "sx", "sy", None),
        P("tm", None, "sx", "sy", None),
        P("tm", None, "sx", "sy", None),
        P("tm", None, "sx", "sy", None),
    )
    out_specs = (
        P("tm", None, "sx", "sy", None),
        P("tm", None, "sx", "sy", None),
        P("tm", None, "sx", "sy", None),
    )
    return jax.shard_map(shards, mesh=mesh, in_specs=in_specs, out_specs=out_specs, check_vma=False)
```

```python
import jax
import jax.numpy as jnp
from jax import lax
from jax.experimental import pallas as pl
from jax.experimental.pallas import tpu as pltpu
from jax.sharding import PartitionSpec as P

F32 = jnp.float32
HIGH = lax.Precision.HIGHEST


def call(body, outs, args, scratch=(), smem=0, limit=24):
    vmem = pl.BlockSpec(memory_space=pltpu.VMEM)
    scalar = pl.BlockSpec(memory_space=pltpu.SMEM)
    single = not isinstance(outs, list)
    shapes = [outs] if single else outs
    got = pl.pallas_call(
        body,
        out_shape=[jax.ShapeDtypeStruct(s, F32) for s in shapes],
        in_specs=[scalar] * smem + [vmem] * (len(args) - smem),
        out_specs=[vmem] * len(shapes),
        scratch_shapes=[pltpu.VMEM(s, F32) for s in scratch],
        compiler_params=pltpu.CompilerParams(vmem_limit_bytes=limit * 2**20),
        name=body.__name__,
    )(*args)
    return got[0] if single else got


def shifted(value, amount, axis):
    return pltpu.roll(value, amount % value.shape[axis], axis)


def nxt(value, step, axis):
    return shifted(value, -step, axis)


def prv(value, step, axis):
    return shifted(value, step, axis)


def index_along(shape, axis):
    return lax.broadcasted_iota(jnp.int32, shape, axis)


def pair_sum(value, step, axis):
    upper = (index_along(value.shape, axis) // step) % 2 == 1
    return value + jnp.where(upper, prv(value, step, axis), nxt(value, step, axis))


def ring_sum(value, step_y, step_z):
    return (
        nxt(value, step_y, 0)
        + prv(value, step_y, 0)
        + nxt(value, step_z, 1)
        + prv(value, step_z, 1)
    )


def restricted_defect(before, first, second, after, step_y, step_z):
    both = first + second
    total = both * (1.0 / 3.0) + (before + both + after + ring_sum(both, step_y, step_z)) * (1.0 / 9.0)
    return pair_sum(pair_sum(total, step_y, 0), step_z, 1) * 0.125


def smoothed(before, here, after, source, spacing_sq, step_y, step_z):
    around = before + after + ring_sum(here, step_y, step_z)
    return here * (1.0 / 3.0) + (around - spacing_sq * source) * (1.0 / 9.0)


def deep_pressure(r3, step_y, step_z):
    r4 = [
        restricted_defect(r3[2 * w], r3[2 * w + 1], r3[2 * w + 2], r3[2 * w + 3], step_y, step_z)
        for w in range(7)
    ]
    low_y, low_z = 2 * step_y, 2 * step_z
    p4 = [r * (-256.0 / 9.0) for r in r4]
    for sweep in range(2):
        inner = range(1 + sweep, 6 - sweep)
        fresh = {w: smoothed(p4[w - 1], p4[w], p4[w + 1], r4[w], 256.0, low_y, low_z) for w in inner}
        p4 = [fresh.get(w) for w in range(7)]
    e3 = {q: r3[q] * (-64.0 / 9.0) + p4[(q - 7) // 2 + 3] for q in range(5, 11)}
    return [
        smoothed(e3[q - 1], e3[q], e3[q + 1], r3[q], 64.0, step_y, step_z) for q in range(6, 10)
    ]


def advected(ref, base, i, comp):
    here = ref[base + comp, i]
    grad_x = ref[base + comp, i + 1] - ref[base + comp, i - 1]
    grad_y = nxt(here, 1, 0) - prv(here, 1, 0)
    grad_z = nxt(here, 1, 1) - prv(here, 1, 1)
    return ref[base, i] * grad_x + ref[base + 1, i] * grad_y + ref[base + 2, i] * grad_z


def z_pick(high):
    k = index_along((128, 128), 0)
    j = index_along((128, 128), 1)
    return jnp.where(k // 2 == j - 64 * high, 1.0, 0.0).astype(F32)


def z_spread(high):
    k = index_along((128, 128), 0)
    j = index_along((128, 128), 1)
    return jnp.where(k == j // 2 + 64 * high, 1.0, 0.0).astype(F32)


def dot(a, b):
    return lax.dot_general(a, b, (((1,), (0,)), ((), ())), precision=HIGH, preferred_element_type=F32)


def restricted_packed(fine, rows, half):
    for comp in range(4):
        for big in range(8):
            rows[comp, big] = fine[comp, 2 * big] + fine[comp, 2 * big + 1]
    for comp in range(4):
        for big in range(8):
            half[comp, big] = rows[comp, big, pl.ds(0, 8, 2), :] + rows[comp, big, pl.ds(1, 8, 2), :]
    low, high = z_pick(0), z_pick(1)
    return [
        0.125
        * (
            dot(half[2 * h].reshape(64, 128), low)
            + dot(half[2 * h + 1].reshape(64, 128), high)
        )
        for h in range(2)
    ]


def opening_body(initial, out, rows, half):
    packed = restricted_packed(initial, rows, half)
    for h in range(2):
        out[h] = packed[h].reshape(8, 8, 128)


def level2_pressure(r2, e2, step_z):
    r3 = [
        restricted_defect(r2[2 * q + 1], r2[2 * q + 2], r2[2 * q + 3], r2[2 * q + 4], 1, step_z)
        for q in range(16)
    ]
    p3 = deep_pressure(r3, 2, 2 * step_z)
    for i in range(8):
        e2[i] = r2[14 + i] * (-16.0 / 9.0) + p3[i // 2]
    return [
        smoothed(e2[i], e2[i + 1], e2[i + 2], r2[15 + i], 16.0, 1, step_z) for i in range(6)
    ]


def bit_lane(value, lane, step, bit):
    same = (lane // step) % 2 == bit
    return jnp.where(same, value, nxt(value, step, 1) if bit else prv(value, step, 1))


def fine_source_body(begin, end, left, right, low, high, comb_out, r0_out, state, comb):
    for f in range(8):
        own = begin if f < 4 else end
        c = f % 4
        state[f, 0:2, 4:20] = left[f]
        state[f, 2:18, 4:20] = own[c]
        state[f, 18:20, 4:20] = right[f]
        state[f, :, 2:4] = low[20 * f : 20 * f + 20]
        state[f, :, 20:22] = high[20 * f : 20 * f + 20]
    for i in range(1, 19):
        for c in range(4):
            total = state[c, i] - 0.125 * (advected(state, 0, i, c) + advected(state, 4, i, c))
            if c == 2:
                total = total + 0.25 * (state[3, i] + state[7, i])
            comb[c, i - 1] = total
    for x in range(16):
        v = comb[1, x + 1]
        w = comb[2, x + 1]
        div = comb[0, x + 2] - comb[0, x] + nxt(v, 1, 0) - prv(v, 1, 0) + nxt(w, 1, 1) - prv(w, 1, 1)
        r0_out[x] = (0.5 * div)[4:20]
        for c in range(4):
            comb_out[c, x] = comb[c, x + 1, 4:20, :]


def fine_down_body(own, below, across, above, coarse, to_left, to_right, r0_out, r0, r1, r2):
    r0[:, 0:16] = below[...]
    r0[:, 16:32] = own[...]
    r0[:, 32:48] = above[...]
    r0[:, 48:64] = across[...]
    r0_out[...] = r0[:, 8:40]
    zero = jnp.zeros((64, 128), F32)

    def at0(x):
        return r0[x] if 0 <= x < 16 else zero

    def at1(x):
        return r1[x + 1] if -1 <= x < 9 else zero

    for x in range(-1, 9):
        r1[x + 1] = restricted_defect(at0(2 * x - 1), at0(2 * x), at0(2 * x + 1), at0(2 * x + 2), 1, 1)
    for x in range(-1, 5):
        r2[x + 1] = restricted_defect(at1(2 * x - 1), at1(2 * x), at1(2 * x + 1), at1(2 * x + 2), 2, 2)
    lane = index_along((16, 128), 1)
    part = [r2[i, pl.ds(0, 16, 4), :] for i in range(6)]
    odd = lane % 2 == 1
    first = jnp.where(
        lane % 4 < 2, jnp.where(odd, part[1], part[0]), jnp.where(odd, part[3], part[2])
    )
    second = jnp.where(odd, part[5], part[4])
    for ref, face in ((to_left, 0), (to_right, 11)):
        ref[0:16] = first
        ref[16:32] = second
        ref[32:48] = coarse[...]
        for i in range(5):
            ref[48 + 32 * i : 80 + 32 * i] = r0[face + i, 8:40]


def fine_up_body(
    tri_l, tri, tri_r, left, own, right, comb, old, fine, rj, r0, r1, r2, e2, p2, e1, p1, e0, p0, rows, half
):
    for i in range(5):
        r0[i] = left[48 + 32 * i : 80 + 32 * i]
        r0[21 + i] = right[48 + 32 * i : 80 + 32 * i]
    r0[5:21] = own[...]
    lane = index_along((16, 128), 1)
    parts = []
    for ref in (tri_l, tri, tri_r):
        for j in range(3):
            first, second = ref[j, 0:16], ref[j, 16:32]
            even, odd = bit_lane(first, lane, 2, 0), bit_lane(first, lane, 2, 1)
            parts.append(
                [
                    bit_lane(even, lane, 1, 0),
                    bit_lane(even, lane, 1, 1),
                    bit_lane(odd, lane, 1, 0),
                    bit_lane(odd, lane, 1, 1),
                    bit_lane(second, lane, 1, 0),
                    bit_lane(second, lane, 1, 1),
                ]
            )
    for j in range(9):
        for n in range(4):
            value = parts[j][n + 1]
            if n == 0 and j > 0:
                value = value + parts[j - 1][5]
            if n == 3 and j < 8:
                value = value + parts[j + 1][0]
            r2[4 * j + n] = value
    for i, value in enumerate(level2_pressure(r2, e2, 4)):
        for y2 in range(8):
            p2[i, 4 * y2 : 4 * y2 + 4, :] = jnp.broadcast_to(value[y2 + 2 : y2 + 3], (4, 128))
    for k in range(12):
        a = 2 * k + 1
        r1[k] = restricted_defect(r0[a - 1], r0[a], r0[a + 1], r0[a + 2], 1, 1)
        e1[k] = r1[k] * (-4.0 / 9.0) + p2[k // 2]
    for k in range(10):
        p1[k] = smoothed(e1[k], e1[k + 1], e1[k + 2], r1[k + 1], 4.0, 2, 2)
    for j in range(20):
        e0[j] = r0[j + 3] * (-1.0 / 9.0) + p1[j // 2]
    for j in range(18):
        p0[j] = smoothed(e0[j], e0[j + 1], e0[j + 2], r0[j + 4], 1.0, 1, 1)
    for x in range(16):
        here = p0[x + 1]
        fine[0, x] = comb[0, x] - 0.5 * (p0[x + 2, 8:24] - p0[x, 8:24])
        fine[1, x] = comb[1, x] - 0.5 * (nxt(here, 1, 0) - prv(here, 1, 0))[8:24]
        mid = here[8:24]
        fine[2, x] = comb[2, x] - 0.5 * (nxt(mid, 1, 1) - prv(mid, 1, 1))
        fine[3, x] = comb[3, x]
    packed = restricted_packed(fine, rows, half)
    for h in range(2):
        rj[h] = packed[h].reshape(8, 8, 128) - old[h]


def coarse_down_body(before, low, high, after, comb_out, r1, message, state, comb, r2):
    lane = index_along((32, 128), 1)
    for side, ref in enumerate((before, low, high, after)):
        for x in range(4):
            for h in range(2):
                pair = ref[h, x]
                other = shifted(pair, 64, 1)
                state[2 * h, 4 * side + x] = jnp.where(lane < 64, pair, other)
                state[2 * h + 1, 4 * side + x] = jnp.where(lane < 64, other, pair)
    for i in range(1, 15):
        for c in range(3):
            total = state[c, i] - 0.125 * advected(state, 0, i, c)
            if c == 2:
                total = total + 0.5 * state[3, i]
            comb[c, i - 1] = total
            if 4 <= i < 12:
                comb_out[c, i - 4] = total
    for x in range(8):
        comb_out[3, x] = state[3, x + 4] - 0.125 * advected(state, 0, x + 4, 3)
    for k in range(12):
        v = comb[1, k + 1]
        w = comb[2, k + 1]
        div = comb[0, k + 2] - comb[0, k] + nxt(v, 1, 0) - prv(v, 1, 0) + nxt(w, 1, 1) - prv(w, 1, 1)
        r1[k] = 0.25 * div
    for m in range(4):
        a = 2 * m + 2
        r2[m] = restricted_defect(r1[a - 1], r1[a], r1[a + 1], r1[a + 2], 1, 1)
    part = [r2[m, pl.ds(0, 16, 2), :] for m in range(4)]
    lane = index_along((16, 128), 1)
    odd = lane % 2 == 1
    message[...] = jnp.where(
        lane < 64, jnp.where(odd, part[1], part[0]), jnp.where(odd, part[3], part[2])
    )


def coarse_up_core(base, tri_l, tri, tri_r, comb, r1, r2, e2, p2, e1, p1, emit):
    lane = index_along((16, 128), 1)
    for side, ref in enumerate((tri_l, tri, tri_r)):
        for j in range(3):
            block = ref[j, base : base + 16]
            other = shifted(block, 64, 1)
            n = 4 * (3 * side + j)
            for m, pair in enumerate(
                (jnp.where(lane < 64, block, other), jnp.where(lane < 64, other, block))
            ):
                r2[n + 2 * m] = bit_lane(pair, lane, 1, 0)
                r2[n + 2 * m + 1] = bit_lane(pair, lane, 1, 1)
    for i, value in enumerate(level2_pressure(r2, e2, 2)):
        p2[i, pl.ds(0, 16, 2), :] = value
        p2[i, pl.ds(1, 16, 2), :] = value
    for k in range(12):
        e1[k] = r1[k] * (-4.0 / 9.0) + p2[k // 2]
    for k in range(10):
        p1[k] = smoothed(e1[k], e1[k + 1], e1[k + 2], r1[k + 1], 4.0, 1, 1)
    lane = index_along((32, 128), 1)
    for x in range(8):
        here = p1[x + 1]
        u = comb[0, x] - 0.25 * (p1[x + 2] - p1[x])
        v = comb[1, x] - 0.25 * (nxt(here, 1, 0) - prv(here, 1, 0))
        w = comb[2, x] - 0.25 * (nxt(here, 1, 1) - prv(here, 1, 1))
        emit(0, x, jnp.where(lane < 64, u, v))
        emit(1, x, jnp.where(lane < 64, w, comb[3, x]))


UP_SCRATCH = [(36, 16, 128), (8, 16, 128), (6, 32, 128), (12, 32, 128), (10, 32, 128)]


def coarse_up_first_body(tri_l, tri, tri_r, comb, r1, ended, *scratch):
    def emit(h, x, value):
        ended[h, x] = value

    coarse_up_core(32, tri_l, tri, tri_r, comb, r1, *scratch, emit)


def coarse_up_next_body(where, tri_l, tri, tri_r, comb, r1, jump, ended, low, high, *scratch):
    def emit(h, x, value):
        scratch[5][h, x] = value
        ref = low if x < 4 else high
        ref[h, x % 4] = value + jump[h, x]

    coarse_up_core(0, tri_l, tri, tri_r, comb, r1, *scratch[:5], emit)
    ended[...] = scratch[5][:, :, rows_of(where, 0), :]


def coarse_up_last_body(where, tri_l, tri, tri_r, comb, r1, e0, e1, e2, out, *scratch):
    def emit(h, x, value):
        scratch[5][h, x] = value

    coarse_up_core(0, tri_l, tri, tri_r, comb, r1, *scratch[:5], emit)
    t = where[2]
    for h in range(2):
        e3 = scratch[5][h, :, rows_of(where, 0), :]
        value = jnp.where(
            t < 2, jnp.where(t == 0, e0[h], e1[h]), jnp.where(t == 2, e2[h], e3)
        )
        out[2 * h] = value[:, :, :64]
        out[2 * h + 1] = shifted(value, 64, 2)[:, :, :64]


def rows_of(where, step):
    return pl.ds(pl.multiple_of(8 * ((where[1] + 4 - step) % 4), 8), 8)


def join_body(where, a0, a1, a2, a3, low, high):
    for step, ref in enumerate((a0, a1, a2, a3)):
        rows = rows_of(where, step)
        for h in range(2):
            for x in range(4):
                low[h, x, rows, :] = ref[h, x]
                high[h, x, rows, :] = ref[h, x + 4]


def join_jumps_body(where, a0, a1, a2, a3, ended, low, high, second, third, own):
    for step, ref in enumerate((a0, a1, a2, a3)):
        rows = rows_of(where, step)
        for h in range(2):
            for x in range(8):
                first = low if x < 4 else high
                first[h, x % 4, rows, :] = ref[0, h, x] + ended[h, x, rows, :]
                second[h, x, rows, :] = ref[1, h, x]
                third[h, x, rows, :] = ref[2, h, x]
    own[...] = ended[:, :, rows_of(where, 0), :]


def new_start_body(where, fine, initial, l1, h1, l2, h2, l3, h3, out, rows, half, tall):
    t = where[2]

    @pl.when(t == 0)
    def _():
        out[...] = initial[...]

    @pl.when(t > 0)
    def _():
        packed = restricted_packed(fine, rows, half)
        mine = rows_of(where, 0)
        for h in range(2):
            for part, (a, b, c) in enumerate(((l1, l2, l3), (h1, h2, h3))):
                state = jnp.where(
                    t == 1, a[h, :, mine, :], jnp.where(t == 2, b[h, :, mine, :], c[h, :, mine, :])
                )
                change = state.reshape(32, 128) - packed[h][32 * part : 32 * part + 32]
                for side in range(2):
                    comp = 2 * h + side
                    wide = dot(change, z_spread(side)).reshape(4, 8, 128)
                    for x in range(4):
                        tall[comp, 4 * part + x, pl.ds(0, 8, 2), :] = wide[x]
                        tall[comp, 4 * part + x, pl.ds(1, 8, 2), :] = wide[x]
        for comp in range(4):
            for x in range(16):
                out[comp, x] = fine[comp, x] + tall[comp, x // 2]


def moved(value, axis, step):
    count = lax.axis_size(axis)
    return lax.ppermute(value, axis, [(i, (i + step) % count) for i in range(count)])


def both_sides(low_face, high_face, axis, step=1):
    return moved(high_face, axis, step), moved(low_face, axis, -step)


def around(value, axis):
    return [moved(value, axis, step) for step in range(1, 4)]


def nine(message):
    left, right = both_sides(message, message, "sx")
    return nine_of(left, message, right)


def nine_of(left, message, right):
    tri = jnp.stack([left, message, right])
    tri_l, tri_r = both_sides(tri, tri, "sx", 3)
    return [tri_l, tri, tri_r]


def shards(initial_state, start_old, end_old, coarse_old):
    begin, end, old = start_old[0], end_old[0], coarse_old[0]
    sx, sy, t = lax.axis_index("sx"), lax.axis_index("sy"), lax.axis_index("tm")
    where = jnp.stack([sx, sy, t]).astype(jnp.int32)

    def face(cut):
        return jnp.concatenate([begin[cut], end[cut]], axis=0)

    every = slice(None)
    left, right = both_sides(face((every, slice(0, 2))), face((every, slice(14, 16))), "sx")
    opening = call(opening_body, (2, 8, 8, 128), [initial_state], [(4, 8, 16, 128), (4, 8, 8, 128)])
    old_packed = jnp.stack(
        [jnp.concatenate([old[0], old[1]], axis=-1), jnp.concatenate([old[2], old[3]], axis=-1)]
    )

    def y_face(cut):
        inner = face((every, every, cut))
        rows = jnp.concatenate([left[:, :, cut], inner, right[:, :, cut]], axis=1)
        return jnp.concatenate([rows.reshape(160, 2, 128), opening.reshape(64, 2, 128)], axis=0)

    low, high = both_sides(y_face(slice(0, 2)), y_face(slice(14, 16)), "sy")
    opening_across = moved(opening, "sy", 2)
    comb, r0 = call(
        fine_source_body,
        [(4, 16, 16, 128), (16, 16, 128)],
        [begin, end, left, right, low, high],
        [(8, 20, 24, 128), (4, 18, 24, 128)],
    )
    r0_below, r0_across, r0_above = around(r0, "sy")

    def opening_of(got):
        return got[160:].reshape(2, 8, 8, 128)

    c0 = call(
        join_body,
        [(2, 4, 32, 128)] * 2,
        [where, opening, opening_of(low), opening_across, opening_of(high)],
        smem=1,
    )

    def coarse_down(state):
        low, high = state
        before, after = both_sides(low, high, "sx")
        return call(
            coarse_down_body,
            [(4, 8, 32, 128), (12, 32, 128), (16, 128)],
            [before, low, high, after],
            [(4, 16, 32, 128), (3, 14, 32, 128), (4, 32, 128)],
        )

    comb0, first0, message0 = coarse_down(c0)

    to_left, to_right, r0_own = call(
        fine_down_body,
        [(208, 128), (208, 128), (16, 32, 128)],
        [r0, r0_below, r0_across, r0_above, message0],
        [(16, 64, 128), (10, 64, 128), (6, 64, 128)],
    )
    from_left, from_right = both_sides(to_left, to_right, "sx")
    tris = nine_of(from_left[:48], to_left[:48], from_right[:48])
    fine_end, rj = call(
        fine_up_body,
        [(4, 16, 16, 128), (2, 8, 8, 128)],
        tris + [from_left, r0_own, from_right, comb, old_packed],
        [
            (26, 32, 128),
            (12, 32, 128),
            (36, 16, 128),
            (8, 16, 128),
            (6, 32, 128),
            (12, 32, 128),
            (10, 32, 128),
            (20, 32, 128),
            (18, 32, 128),
            (4, 8, 16, 128),
            (4, 8, 8, 128),
        ],
    )

    turned = [rj] + around(rj, "tm")
    ended0 = call(coarse_up_first_body, (2, 8, 32, 128), tris + [comb0, first0], UP_SCRATCH)

    def slice_of(s):
        back = (t - s) % 4
        return jnp.where(
            back < 2,
            jnp.where(back == 0, turned[0], turned[1]),
            jnp.where(back == 2, turned[2], turned[3]),
        )

    jumps = jnp.stack([slice_of(s) for s in range(3)])
    low1, high1, jump1, jump2, own0 = call(
        join_jumps_body,
        [(2, 4, 32, 128)] * 2 + [(2, 8, 32, 128)] * 2 + [(2, 8, 8, 128)],
        [where, jumps] + around(jumps, "sy") + [ended0],
        smem=1,
    )
    c1 = [low1, high1]
    fine_before = moved(fine_end, "tm", 1)

    def coarse_step(state, jump):
        combined, level1, message = coarse_down(state)
        own, low, high = call(
            coarse_up_next_body,
            [(2, 8, 8, 128)] + [(2, 4, 32, 128)] * 2,
            [where] + nine(message) + [combined, level1, jump],
            UP_SCRATCH + [(2, 8, 32, 128)],
            smem=1,
        )
        return own, [low, high]

    own1, c2 = coarse_step(c1, jump1)
    own2, c3 = coarse_step(c2, jump2)
    new_start = call(
        new_start_body,
        (4, 16, 16, 128),
        [where, fine_before, initial_state] + c1 + c2 + c3,
        [(4, 8, 16, 128), (4, 8, 8, 128), (4, 8, 16, 128)],
        smem=1,
    )
    combined, level1, message = coarse_down(c3)
    coarse_end = call(
        coarse_up_last_body,
        (4, 8, 8, 64),
        [where] + nine(message) + [combined, level1, own0, own1, own2],
        UP_SCRATCH + [(2, 8, 32, 128)],
        smem=1,
    )
    return (new_start[None], fine_end[None], coarse_end[None])


def solution(mesh):
    in_specs = (
        P(None, "sx", "sy", None),
        P("tm", None, "sx", "sy", None),
        P("tm", None, "sx", "sy", None),
        P("tm", None, "sx", "sy", None),
    )
    out_specs = (
        P("tm", None, "sx", "sy", None),
        P("tm", None, "sx", "sy", None),
        P("tm", None, "sx", "sy", None),
    )
    return jax.shard_map(shards, mesh=mesh, in_specs=in_specs, out_specs=out_specs, check_vma=False)
```

```python
import jax
import jax.numpy as jnp
from jax import lax
from jax.experimental import pallas as pl
from jax.experimental.pallas import tpu as pltpu
from jax.sharding import PartitionSpec as P

F32 = jnp.float32
HIGH = lax.Precision.HIGHEST


def call(body, outs, args, scratch=(), smem=0, limit=24, far=False):
    vmem = pl.BlockSpec(memory_space=pltpu.VMEM)
    scalar = pl.BlockSpec(memory_space=pltpu.SMEM)
    single = not isinstance(outs, list)
    shapes = [outs] if single else outs
    got = pl.pallas_call(
        body,
        out_shape=[jax.ShapeDtypeStruct(s, F32) for s in shapes],
        in_specs=[scalar] * smem
        + [pl.BlockSpec(memory_space=pl.ANY) if far else vmem] * (len(args) - smem),
        out_specs=[vmem] * len(shapes),
        scratch_shapes=[pltpu.VMEM(s, F32) for s in scratch]
        + ([pltpu.SemaphoreType.DMA((3, 4))] if far else []),
        compiler_params=pltpu.CompilerParams(vmem_limit_bytes=limit * 2**20),
        name=body.__name__,
    )(*args)
    return got[0] if single else got


def shifted(value, amount, axis):
    return pltpu.roll(value, amount % value.shape[axis], axis)


def nxt(value, step, axis):
    return shifted(value, -step, axis)


def prv(value, step, axis):
    return shifted(value, step, axis)


def index_along(shape, axis):
    return lax.broadcasted_iota(jnp.int32, shape, axis)


def pair_sum(value, step, axis):
    upper = (index_along(value.shape, axis) // step) % 2 == 1
    return value + jnp.where(upper, prv(value, step, axis), nxt(value, step, axis))


def ring_sum(value, step_y, step_z):
    return (
        nxt(value, step_y, 0)
        + prv(value, step_y, 0)
        + nxt(value, step_z, 1)
        + prv(value, step_z, 1)
    )


def restricted_defect(before, first, second, after, step_y, step_z):
    both = first + second
    total = both * (1.0 / 3.0) + (before + both + after + ring_sum(both, step_y, step_z)) * (1.0 / 9.0)
    return pair_sum(pair_sum(total, step_y, 0), step_z, 1) * 0.125


def smoothed(before, here, after, source, spacing_sq, step_y, step_z):
    around = before + after + ring_sum(here, step_y, step_z)
    return here * (1.0 / 3.0) + (around - spacing_sq * source) * (1.0 / 9.0)


def deep_pressure(r3, step_y, step_z):
    r4 = [
        restricted_defect(r3[2 * w], r3[2 * w + 1], r3[2 * w + 2], r3[2 * w + 3], step_y, step_z)
        for w in range(7)
    ]
    low_y, low_z = 2 * step_y, 2 * step_z
    p4 = [r * (-256.0 / 9.0) for r in r4]
    for sweep in range(2):
        inner = range(1 + sweep, 6 - sweep)
        fresh = {w: smoothed(p4[w - 1], p4[w], p4[w + 1], r4[w], 256.0, low_y, low_z) for w in inner}
        p4 = [fresh.get(w) for w in range(7)]
    e3 = {q: r3[q] * (-64.0 / 9.0) + p4[(q - 7) // 2 + 3] for q in range(5, 11)}
    return [
        smoothed(e3[q - 1], e3[q], e3[q + 1], r3[q], 64.0, step_y, step_z) for q in range(6, 10)
    ]


def advected(ref, i, comp):
    here = ref[comp, i]
    grad_x = ref[comp, i + 1] - ref[comp, i - 1]
    grad_y = nxt(here, 1, 0) - prv(here, 1, 0)
    grad_z = nxt(here, 1, 1) - prv(here, 1, 1)
    return ref[0, i] * grad_x + ref[1, i] * grad_y + ref[2, i] * grad_z


def z_pick(high):
    k = index_along((128, 128), 0)
    j = index_along((128, 128), 1)
    return jnp.where(k // 2 == j - 64 * high, 1.0, 0.0).astype(F32)


def z_spread(high):
    k = index_along((128, 128), 0)
    j = index_along((128, 128), 1)
    return jnp.where(k == j // 2 + 64 * high, 1.0, 0.0).astype(F32)


def dot(a, b):
    return lax.dot_general(a, b, (((1,), (0,)), ((), ())), precision=HIGH, preferred_element_type=F32)


def packed_pairs(half, rows):
    low, high = z_pick(0), z_pick(1)
    packed = []
    for h in range(2):
        value = dot(half[2 * h].reshape(rows, 128), low)
        if 2 * h + 1 < half.shape[0]:
            value = value + dot(half[2 * h + 1].reshape(rows, 128), high)
        packed.append(0.125 * value)
    return packed


def restricted_packed(fine, rows, half):
    for comp in range(4):
        for big in range(8):
            rows[comp, big] = fine[comp, 2 * big] + fine[comp, 2 * big + 1]
    for comp in range(4):
        for big in range(8):
            half[comp, big] = rows[comp, big, pl.ds(0, 8, 2), :] + rows[comp, big, pl.ds(1, 8, 2), :]
    return packed_pairs(half, 64)


def pack_body(
    initial_far, begin_far, end_far, x_low, x_high, y_low, y_high, opening,
    rows, half, initial, begin, end, arrived
):
    copies = [
        pltpu.make_async_copy(far.at[c], near.at[c], arrived.at[n, c])
        for n, (far, near) in enumerate(
            ((begin_far, begin), (end_far, end), (initial_far, initial))
        )
        for c in range(4)
    ]
    for copy in copies:
        copy.start()
    for copy in copies[:8]:
        copy.wait()
    for f in range(8):
        ref = begin if f < 4 else end
        x_low[f] = ref[f % 4, 0]
        x_high[f] = ref[f % 4, 15]
        for x in range(16):
            y_low[f, x : x + 1, :] = ref[f % 4, x, 0:1, :]
            y_high[f, x : x + 1, :] = ref[f % 4, x, 15:16, :]
    for copy in copies[8:]:
        copy.wait()
    packed = restricted_packed(initial, rows, half)
    for h in range(2):
        for x in range(4):
            block = packed[h][16 * x : 16 * x + 16]
            opening[4 * h + x] = block
            y_low[8 + 4 * h + x] = block
            y_high[8 + 4 * h + x] = block


def join_body(below, own, above, across, low, high):
    for b, (ref, first) in enumerate(((below, 8), (own, 0), (above, 8), (across, 0))):
        for h in range(2):
            for x in range(8):
                side = low if x < 4 else high
                side[h, x % 4, 8 * b : 8 * b + 8, :] = ref[
                    first + 4 * h + x // 2, 8 * (x % 2) : 8 * (x % 2) + 8
                ]


def level2_pressure(r2, first, e2, step_z):
    r3 = [
        restricted_defect(
            r2[first + 2 * q + 1], r2[first + 2 * q + 2], r2[first + 2 * q + 3], r2[first + 2 * q + 4], 1, step_z
        )
        for q in range(16)
    ]
    p3 = deep_pressure(r3, 2, 2 * step_z)
    for i in range(8):
        e2[i] = r2[first + 14 + i] * (-16.0 / 9.0) + p3[i // 2]
    return [
        smoothed(e2[i], e2[i + 1], e2[i + 2], r2[first + 15 + i], 16.0, 1, step_z) for i in range(6)
    ]


def ordered(where, got, rows, base, size, blocks):
    own, partner, near, far, swapped = got
    k = where[1]
    blocks[4 + k, 0:size] = own[base : base + size]
    blocks[5 - k, 0:size] = partner[base : base + size]
    for j in range(2):
        low = rows * j + base
        turn = j * (2 * k - 1)
        blocks[3 + 3 * k + turn, 0:size] = near[low : low + size]
        blocks[1 + 7 * k + turn, 0:size] = far[low : low + size]
        blocks[6 - 3 * k - turn, 0:size] = swapped[low : low + size]
        blocks[8 - 7 * k - turn, 0:size] = swapped[2 * rows + low : 2 * rows + low + size]


def bit_lane(value, lane, step, bit):
    same = (lane // step) % 2 == bit
    return jnp.where(same, value, nxt(value, step, 1) if bit else prv(value, step, 1))


def fine_source_body(begin, end, left, right, low, high, old, comb, out, rows, half):
    row = index_along((16, 128), 0)
    first, last = row == 0, row == 15

    def at(f, x):
        if x < 0:
            return left[f]
        if x > 15:
            return right[f]
        return (begin if f < 4 else end)[f % 4, x]

    def carried(f, x):
        base = f - f % 4
        here = at(f, x)
        grad_x = at(f, x + 1) - at(f, x - 1)
        above = jnp.where(last, high[f, x : x + 1, :], nxt(here, 1, 0))
        below = jnp.where(first, low[f, x : x + 1, :], prv(here, 1, 0))
        grad_z = nxt(here, 1, 1) - prv(here, 1, 1)
        return at(base, x) * grad_x + at(base + 1, x) * (above - below) + at(base + 2, x) * grad_z

    for x in range(16):
        for c in range(4):
            total = begin[c, x] - 0.125 * (carried(c, x) + carried(c + 4, x))
            if c == 2:
                total = total + 0.25 * (begin[3, x] + end[3, x])
            comb[c, x] = total
    out[0] = 0.5 * comb[0, 0]
    out[17] = -0.5 * comb[0, 15]
    for x in range(16):
        v = comb[1, x]
        w = comb[2, x]
        div = jnp.where(last, 0.0, nxt(v, 1, 0)) - jnp.where(first, 0.0, prv(v, 1, 0))
        div = div + nxt(w, 1, 1) - prv(w, 1, 1)
        if x < 15:
            div = div + comb[0, x + 1]
        if x > 0:
            div = div - comb[0, x - 1]
        out[x + 1] = 0.5 * div
        out[18, x : x + 1, :] = 0.5 * v[0:1]
        out[19, x : x + 1, :] = -0.5 * v[15:16]
    packed = restricted_packed(comb, rows, half)
    for h in range(2):
        for x in range(4):
            out[20 + 4 * h + x, 0:8] = packed[h][16 * x : 16 * x + 8] - old[h, 2 * x]
            out[20 + 4 * h + x, 8:16] = packed[h][16 * x + 8 : 16 * x + 16] - old[h, 2 * x + 1]


def fine_down_body(
    where, below, own, above, across, coarse,
    message, inner, outer, r0, r1, r2
):
    blocks = (below, own, above, across)
    for b, ref in enumerate(blocks):
        r0[:, 16 * b : 16 * b + 16] = ref[0:18]
    message[32:48] = coarse[...]
    for b in range(4):
        upper, lower = blocks[(b + 1) % 4], blocks[(b + 3) % 4]
        for x in range(16):
            r0[x + 1, 16 * b + 15 : 16 * b + 16] += upper[18, x : x + 1, :]
            r0[x + 1, 16 * b : 16 * b + 1] += lower[19, x : x + 1, :]
    zero = jnp.zeros((64, 128), F32)

    def at0(x):
        return r0[x + 1] if -1 <= x < 17 else zero

    def at1(x):
        return r1[x + 1] if -1 <= x < 9 else zero

    for x in range(-1, 9):
        r1[x + 1] = restricted_defect(at0(2 * x - 1), at0(2 * x), at0(2 * x + 1), at0(2 * x + 2), 1, 1)
    for x in range(-1, 5):
        r2[x + 1] = restricted_defect(at1(2 * x - 1), at1(2 * x), at1(2 * x + 1), at1(2 * x + 2), 2, 2)
    lane = index_along((16, 128), 1)
    part = [r2[i, pl.ds(0, 16, 4), :] for i in range(6)]
    odd = lane % 2 == 1
    first = jnp.where(
        lane % 4 < 2, jnp.where(odd, part[1], part[0]), jnp.where(odd, part[3], part[2])
    )
    second = jnp.where(odd, part[5], part[4])
    message[0:16] = first
    message[16:32] = second
    k = where[1]
    for i in range(6):
        inner[64 * i : 64 * i + 64] = r0[12 - 12 * k + i]
        outer[64 * i : 64 * i + 64] = r0[12 * k + i]


def fine_up_body(
    where, own, partner, near, far, swapped, face_in, face_out, mine, comb, below, own_share, above, across_jump, fine, jump,
    r0, r1, r2, e2, p2, e1, p1, e0, p0, rows, half, blocks
):
    k = where[1]
    ordered(where, (own, partner, near, far, swapped), 48, 0, 32, blocks)
    r0[5:21] = mine[1:17]
    for i in range(6):
        inside = face_in[64 * i : 64 * i + 64]
        outside = face_out[64 * i : 64 * i + 64]
        left = jnp.where(k == 0, outside, inside)
        right = jnp.where(k == 0, inside, outside)
        if i < 5:
            r0[i] = left
        else:
            r0[5] += left
        if i > 0:
            r0[20 + i] = right
        else:
            r0[20] += right
    r0[4] += mine[0]
    r0[21] += mine[17]
    lane = index_along((16, 128), 1)
    parts = []
    for j in range(10):
        first, second = blocks[j, 0:16], blocks[j, 16:32]
        even, odd = bit_lane(first, lane, 2, 0), bit_lane(first, lane, 2, 1)
        parts.append(
            [
                bit_lane(even, lane, 1, 0),
                bit_lane(even, lane, 1, 1),
                bit_lane(odd, lane, 1, 0),
                bit_lane(odd, lane, 1, 1),
                bit_lane(second, lane, 1, 0),
                bit_lane(second, lane, 1, 1),
            ]
        )
    for j in range(10):
        for n in range(4):
            value = parts[j][n + 1]
            if n == 0 and j > 0:
                value = value + parts[j - 1][5]
            if n == 3 and j < 9:
                value = value + parts[j + 1][0]
            r2[4 * j + n] = value
    for i, value in enumerate(level2_pressure(r2, 4 * k, e2, 4)):
        for y2 in range(16):
            p2[i, 4 * y2 : 4 * y2 + 4, :] = jnp.broadcast_to(value[y2 : y2 + 1], (4, 128))
    for k in range(12):
        a = 2 * k + 1
        r1[k] = restricted_defect(r0[a - 1], r0[a], r0[a + 1], r0[a + 2], 1, 1)
        e1[k] = r1[k] * (-4.0 / 9.0) + p2[k // 2]
    for k in range(10):
        p1[k] = smoothed(e1[k], e1[k + 1], e1[k + 2], r1[k + 1], 4.0, 2, 2)
    for j in range(20):
        e0[j] = r0[j + 3] * (-1.0 / 9.0) + p1[j // 2]
    for j in range(18):
        p0[j] = smoothed(e0[j], e0[j + 1], e0[j + 2], r0[j + 4], 1.0, 1, 1)
    for big in range(8):
        a = 2 * big + 1
        pair = p0[a] + p0[a + 1]
        rows[0, big] = p0[a + 1] + p0[a + 2] - p0[a - 1] - p0[a]
        rows[1, big] = nxt(pair, 1, 0) - prv(pair, 1, 0)
        rows[2, big] = nxt(pair, 1, 1) - prv(pair, 1, 1)
    for c in range(3):
        for big in range(8):
            half[c, big] = rows[c, big, pl.ds(0, 32, 2), :] + rows[c, big, pl.ds(1, 32, 2), :]
    packed = packed_pairs(half, 256)
    for h in range(2):
        slope = 0.5 * packed[h].reshape(8, 32, 128)
        for b, (ref, first) in enumerate(((below, 20), (own_share, 20), (above, 20), (across_jump, 0))):
            for x in range(8):
                jump[h, x, 8 * b : 8 * b + 8] = (
                    ref[first + 4 * h + x // 2, 8 * (x % 2) : 8 * (x % 2) + 8]
                    - slope[x, 8 * b : 8 * b + 8]
                )
    for x in range(16):
        here = p0[x + 1, 8:40]
        fine[0, x] = comb[0, x] - 0.5 * (p0[x + 2, 16:32] - p0[x, 16:32])
        fine[1, x] = comb[1, x] - 0.5 * (nxt(here, 1, 0) - prv(here, 1, 0))[8:24]
        mid = here[8:24]
        fine[2, x] = comb[2, x] - 0.5 * (nxt(mid, 1, 1) - prv(mid, 1, 1))
        fine[3, x] = comb[3, x]


def coarse_down_body(before, low, high, after, comb_out, r1, message, state, comb, r2):
    lane = index_along((32, 128), 1)
    for side, ref in enumerate((before, low, high, after)):
        for x in range(4):
            for h in range(2):
                pair = ref[h, x]
                other = shifted(pair, 64, 1)
                state[2 * h, 4 * side + x] = jnp.where(lane < 64, pair, other)
                state[2 * h + 1, 4 * side + x] = jnp.where(lane < 64, other, pair)
    message[...] = coarse_down_core(comb_out, r1, state, comb, r2)


def coarse_down_core(comb_out, r1, state, comb, r2):
    for i in range(1, 15):
        for c in range(3):
            total = state[c, i] - 0.125 * advected(state, i, c)
            if c == 2:
                total = total + 0.5 * state[3, i]
            comb[c, i - 1] = total
            if 4 <= i < 12:
                comb_out[c, i - 4] = total
    for x in range(8):
        comb_out[3, x] = state[3, x + 4] - 0.125 * advected(state, x + 4, 3)
    for k in range(12):
        v = comb[1, k + 1]
        w = comb[2, k + 1]
        div = comb[0, k + 2] - comb[0, k] + nxt(v, 1, 0) - prv(v, 1, 0) + nxt(w, 1, 1) - prv(w, 1, 1)
        r1[k] = 0.25 * div
    for m in range(4):
        a = 2 * m + 2
        r2[m] = restricted_defect(r1[a - 1], r1[a], r1[a + 1], r1[a + 2], 1, 1)
    part = [r2[m, pl.ds(0, 16, 2), :] for m in range(4)]
    lane = index_along((16, 128), 1)
    odd = lane % 2 == 1
    return jnp.where(
        lane < 64, jnp.where(odd, part[1], part[0]), jnp.where(odd, part[3], part[2])
    )


def coarse_up_core(where, rows, base, got, comb, r1, blocks, r2, e2, p2, e1, p1, emit):
    ordered(where, got, rows, base, 16, blocks)
    lane = index_along((16, 128), 1)
    for j in range(10):
        block = blocks[j]
        other = shifted(block, 64, 1)
        for m, pair in enumerate(
            (jnp.where(lane < 64, block, other), jnp.where(lane < 64, other, block))
        ):
            r2[4 * j + 2 * m] = bit_lane(pair, lane, 1, 0)
            r2[4 * j + 2 * m + 1] = bit_lane(pair, lane, 1, 1)
    for i, value in enumerate(level2_pressure(r2, 4 * where[1], e2, 2)):
        p2[i, pl.ds(0, 16, 2), :] = value
        p2[i, pl.ds(1, 16, 2), :] = value
    for k in range(12):
        e1[k] = r1[k] * (-4.0 / 9.0) + p2[k // 2]
    for k in range(10):
        p1[k] = smoothed(e1[k], e1[k + 1], e1[k + 2], r1[k + 1], 4.0, 1, 1)
    lane = index_along((32, 128), 1)
    for x in range(8):
        here = p1[x + 1]
        u = comb[0, x] - 0.25 * (p1[x + 2] - p1[x])
        v = comb[1, x] - 0.25 * (nxt(here, 1, 0) - prv(here, 1, 0))
        w = comb[2, x] - 0.25 * (nxt(here, 1, 1) - prv(here, 1, 1))
        emit(0, x, jnp.where(lane < 64, u, v))
        emit(1, x, jnp.where(lane < 64, w, comb[3, x]))


UP_SCRATCH = [(10, 16, 128), (40, 16, 128), (8, 16, 128), (6, 32, 128), (12, 32, 128), (10, 32, 128)]


def coarse_up_next_body(
    rows, base, where, a, b, c, d, e, comb, r1, jump, ended, own, low, high, *scratch
):
    def emit(h, x, value):
        after = value + jump[h, x]
        ref = low if x < 4 else high
        ref[h, x % 4] = after
        ended[h, x] = value[8:16]
        own[h, x] = after[8:16]

    coarse_up_core(where, rows, base, (a, b, c, d, e), comb, r1, *scratch, emit)


def coarse_up_first_body(*refs):
    coarse_up_next_body(48, 32, *refs)


def coarse_up_middle_body(*refs):
    coarse_up_next_body(16, 0, *refs)


def coarse_up_last_body(where, a, b, c, d, e, comb, r1, ended, *scratch):
    def emit(h, x, value):
        ended[h, x] = value[8:16]

    coarse_up_core(where, 16, 0, (a, b, c, d, e), comb, r1, *scratch, emit)


def new_start_body(where, fine, initial, state, out, rows, half, tall):
    t = where[0]

    @pl.when(t == 0)
    def _():
        out[...] = initial[...]

    @pl.when(t > 0)
    def _():
        packed = restricted_packed(fine, rows, half)
        for h in range(2):
            change = state[h].reshape(64, 128) - packed[h]
            for side in range(2):
                comp = 2 * h + side
                wide = dot(change, z_spread(side)).reshape(8, 8, 128)
                for x in range(8):
                    tall[comp, x, pl.ds(0, 8, 2), :] = wide[x]
                    tall[comp, x, pl.ds(1, 8, 2), :] = wide[x]
        for comp in range(4):
            for x in range(16):
                out[comp, x] = fine[comp, x] + tall[comp, x // 2]


def coarse_end_body(where, e0, e1, e2, e3, out):
    t = where[0]
    for h in range(2):
        low = jnp.where(t == 0, e0[h], e1[h])
        high = jnp.where(t == 2, e2[h], e3[h])
        value = jnp.where(t < 2, low, high)
        out[2 * h] = value[:, :, :64]
        out[2 * h + 1] = shifted(value, 64, 2)[:, :, :64]


def moved(value, axis, step):
    count = lax.axis_size(axis)
    return lax.ppermute(value, axis, [(i, (i + step) % count) for i in range(count)])


def both_sides(low_face, high_face, axis, step=1):
    return moved(high_face, axis, step), moved(low_face, axis, -step)


def around(value, axis):
    return [moved(value, axis, step) for step in range(1, 4)]


def swapped_cores(value):
    return lax.ppermute(value, "sx", [(i, i ^ 1) for i in range(lax.axis_size("sx"))])


def from_chips(value, chips):
    count = lax.axis_size("sx")
    far = 2 * chips - 1
    return lax.ppermute(
        value, "sx", [(i, (i + (far if i % 2 else -far)) % count) for i in range(count)]
    )


def five_chips(message):
    partner = swapped_cores(message)
    both = jnp.concatenate([message, partner], axis=0)
    near, far = from_chips(both, 1), from_chips(both, 2)
    return [message, partner, near, far, swapped_cores(jnp.concatenate([near, far], axis=0))]


def sent(value, source, target):
    return lax.ppermute(value, "tm", [(source, target)])


def shards(initial_state, start_old, end_old, coarse_old):
    begin, end, old = start_old[0], end_old[0], coarse_old[0]
    where = jnp.stack([lax.axis_index("tm"), lax.axis_index("sx") % 2]).astype(jnp.int32)

    x_low, x_high, y_low, y_high, opening = call(
        pack_body,
        [(8, 16, 128)] * 2 + [(16, 16, 128)] * 2 + [(8, 16, 128)],
        [initial_state, begin, end],
        [(4, 8, 16, 128), (4, 8, 8, 128)] + [(4, 16, 16, 128)] * 3,
        limit=56,
        far=True,
    )
    old_packed = jnp.stack(
        [jnp.concatenate([old[0], old[1]], axis=-1), jnp.concatenate([old[2], old[3]], axis=-1)]
    )
    left, right = both_sides(x_low, x_high, "sx")
    low, high = both_sides(y_low, y_high, "sy")
    opening_across = moved(opening, "sy", 2)
    comb, share = call(
        fine_source_body,
        [(4, 16, 16, 128), (28, 16, 128)],
        [begin, end, left, right, low, high, old_packed],
        [(4, 8, 16, 128), (4, 8, 8, 128)],
    )
    c0 = call(join_body, [(2, 4, 32, 128)] * 2, [low, opening, high, opening_across])
    share, c0 = lax.optimization_barrier((share, c0))
    below, above = both_sides(share, share, "sy")
    across = moved(share[:20], "sy", 2)

    def coarse_down(state):
        low, high = state
        before, after = both_sides(low, high, "sx")
        return call(
            coarse_down_body,
            [(4, 8, 32, 128), (12, 32, 128), (16, 128)],
            [before, low, high, after],
            [(4, 16, 32, 128), (3, 14, 32, 128), (4, 32, 128)],
        )

    comb0, first0, message0 = coarse_down(c0)
    message, inner, outer, r0 = call(
        fine_down_body,
        [(48, 128), (384, 128), (384, 128), (18, 64, 128)],
        [where, below, share, above, across, message0],
        [(10, 64, 128), (6, 64, 128)],
        smem=1,
    )
    across_jump = moved(share[20:], "sy", 2)
    partner = swapped_cores(jnp.concatenate([message, inner], axis=0))
    both = jnp.concatenate([message, partner[:48]], axis=0)
    near, far = from_chips(jnp.concatenate([both, outer], axis=0), 1), from_chips(both, 2)
    near, far, across_jump = lax.optimization_barrier((near, far, across_jump))
    crossed = swapped_cores(jnp.concatenate([near[:96], far], axis=0))
    got = [message, partner, near, far, crossed]
    fine_end, jump0 = call(
        fine_up_body,
        [(4, 16, 16, 128), (2, 8, 32, 128)],
        [where] + got + [partner[48:], near[96:], r0, comb, below, share, above, across_jump],
        [
            (26, 64, 128),
            (12, 64, 128),
            (40, 16, 128),
            (8, 16, 128),
            (6, 64, 128),
            (12, 64, 128),
            (10, 64, 128),
            (20, 64, 128),
            (18, 64, 128),
            (3, 8, 64, 128),
            (3, 8, 32, 128),
            (10, 32, 128),
        ],
        smem=1,
    )

    def coarse_up(body, got, combined, level1, jump):
        ended, own, low, high = call(
            body,
            [(2, 8, 8, 128)] * 2 + [(2, 4, 32, 128)] * 2,
            [where] + got + [combined, level1, jump],
            UP_SCRATCH,
            smem=1,
        )
        return ended, own, [low, high]

    ended0, own1, c1 = coarse_up(coarse_up_first_body, got, comb0, first0, jump0)
    jump1 = lax.ppermute(jump0, "tm", [(1, 0), (2, 1)])
    fine_before = moved(fine_end, "tm", 1)

    combined, level1, message = coarse_down(c1)
    got, jump1 = lax.optimization_barrier((five_chips(message), jump1))
    ended1, own2, c2 = coarse_up(coarse_up_middle_body, got, combined, level1, jump1)

    combined, level1, message = coarse_down(c2)
    jump2 = sent(jump1, 1, 0)
    hand1 = sent(jnp.concatenate([own1, ended1], axis=0), 0, 1)
    got, hand1, jump2, fine_before = lax.optimization_barrier(
        (five_chips(message), hand1, jump2, fine_before)
    )
    ended2, own3, c3 = coarse_up(coarse_up_middle_body, got, combined, level1, jump2)

    combined, level1, message = coarse_down(c3)
    hand2 = sent(jnp.concatenate([own2, ended2], axis=0), 0, 2)
    hand3 = sent(own3, 0, 3)
    got, hand2, hand3 = lax.optimization_barrier((five_chips(message), hand2, hand3))
    ended3 = call(
        coarse_up_last_body,
        (2, 8, 8, 128),
        [where] + got + [combined, level1],
        UP_SCRATCH,
        smem=1,
    )
    new_start = call(
        new_start_body,
        (4, 16, 16, 128),
        [where, fine_before, initial_state, hand1[:2] + hand2[:2] + hand3],
        [(4, 8, 16, 128), (4, 8, 8, 128), (4, 8, 16, 128)],
        smem=1,
    )
    coarse_end = call(
        coarse_end_body,
        (4, 8, 8, 64),
        [where, ended0, hand1[2:], hand2[2:], sent(ended3, 0, 3)],
        smem=1,
    )
    return (new_start[None], fine_end[None], coarse_end[None])


def solution(mesh):
    in_specs = (
        P(None, "sx", "sy", None),
        P("tm", None, "sx", "sy", None),
        P("tm", None, "sx", "sy", None),
        P("tm", None, "sx", "sy", None),
    )
    out_specs = (
        P("tm", None, "sx", "sy", None),
        P("tm", None, "sx", "sy", None),
        P("tm", None, "sx", "sy", None),
    )
    return jax.shard_map(shards, mesh=mesh, in_specs=in_specs, out_specs=out_specs, check_vma=False)
```

```python
import jax
import jax.numpy as jnp
from jax import lax
from jax.experimental import pallas as pl
from jax.experimental.pallas import tpu as pltpu
from jax.sharding import PartitionSpec as P

F32 = jnp.float32
HIGH = lax.Precision.HIGHEST


def call(body, outs, args, scratch=(), smem=0, limit=24, far=False):
    vmem = pl.BlockSpec(memory_space=pltpu.VMEM)
    scalar = pl.BlockSpec(memory_space=pltpu.SMEM)
    single = not isinstance(outs, list)
    shapes = [outs] if single else outs
    got = pl.pallas_call(
        body,
        out_shape=[jax.ShapeDtypeStruct(s, F32) for s in shapes],
        in_specs=[scalar] * smem
        + [pl.BlockSpec(memory_space=pl.ANY) if far else vmem] * (len(args) - smem),
        out_specs=[vmem] * len(shapes),
        scratch_shapes=[pltpu.VMEM(s, F32) for s in scratch]
        + ([pltpu.SemaphoreType.DMA((3, 4))] if far else []),
        compiler_params=pltpu.CompilerParams(vmem_limit_bytes=limit * 2**20),
        name=body.__name__,
    )(*args)
    return got[0] if single else got


def shifted(value, amount, axis):
    return pltpu.roll(value, amount % value.shape[axis], axis)


def nxt(value, step, axis):
    return shifted(value, -step, axis)


def prv(value, step, axis):
    return shifted(value, step, axis)


def index_along(shape, axis):
    return lax.broadcasted_iota(jnp.int32, shape, axis)


def pair_sum(value, step, axis):
    upper = (index_along(value.shape, axis) // step) % 2 == 1
    return value + jnp.where(upper, prv(value, step, axis), nxt(value, step, axis))


def ring_sum(value, step_y, step_z):
    return (
        nxt(value, step_y, 0)
        + prv(value, step_y, 0)
        + nxt(value, step_z, 1)
        + prv(value, step_z, 1)
    )


def restricted_defect(before, first, second, after, step_y, step_z):
    both = first + second
    total = both * (1.0 / 3.0) + (before + both + after + ring_sum(both, step_y, step_z)) * (1.0 / 9.0)
    return pair_sum(pair_sum(total, step_y, 0), step_z, 1) * 0.125


def smoothed(before, here, after, source, spacing_sq, step_y, step_z):
    around = before + after + ring_sum(here, step_y, step_z)
    return here * (1.0 / 3.0) + (around - spacing_sq * source) * (1.0 / 9.0)


def deep_pressure(r3, step_y, step_z):
    r4 = [
        restricted_defect(r3[2 * w], r3[2 * w + 1], r3[2 * w + 2], r3[2 * w + 3], step_y, step_z)
        for w in range(7)
    ]
    low_y, low_z = 2 * step_y, 2 * step_z
    p4 = [r * (-256.0 / 9.0) for r in r4]
    for sweep in range(2):
        inner = range(1 + sweep, 6 - sweep)
        fresh = {w: smoothed(p4[w - 1], p4[w], p4[w + 1], r4[w], 256.0, low_y, low_z) for w in inner}
        p4 = [fresh.get(w) for w in range(7)]
    e3 = {q: r3[q] * (-64.0 / 9.0) + p4[(q - 7) // 2 + 3] for q in range(5, 11)}
    return [
        smoothed(e3[q - 1], e3[q], e3[q + 1], r3[q], 64.0, step_y, step_z) for q in range(6, 10)
    ]


def advected(ref, i, comp):
    here = ref[comp, i]
    grad_x = ref[comp, i + 1] - ref[comp, i - 1]
    grad_y = nxt(here, 1, 0) - prv(here, 1, 0)
    grad_z = nxt(here, 1, 1) - prv(here, 1, 1)
    return ref[0, i] * grad_x + ref[1, i] * grad_y + ref[2, i] * grad_z


def z_pick(high):
    k = index_along((128, 128), 0)
    j = index_along((128, 128), 1)
    return jnp.where(k // 2 == j - 64 * high, 1.0, 0.0).astype(F32)


def z_spread(high):
    k = index_along((128, 128), 0)
    j = index_along((128, 128), 1)
    return jnp.where(k == j // 2 + 64 * high, 1.0, 0.0).astype(F32)


def dot(a, b):
    return lax.dot_general(a, b, (((1,), (0,)), ((), ())), precision=HIGH, preferred_element_type=F32)


def packed_pairs(half, rows):
    low, high = z_pick(0), z_pick(1)
    packed = []
    for h in range(2):
        value = dot(half[2 * h].reshape(rows, 128), low)
        if 2 * h + 1 < half.shape[0]:
            value = value + dot(half[2 * h + 1].reshape(rows, 128), high)
        packed.append(0.125 * value)
    return packed


def restricted_packed(fine, rows, half):
    for comp in range(4):
        for big in range(8):
            rows[comp, big] = fine[comp, 2 * big] + fine[comp, 2 * big + 1]
    for comp in range(4):
        for big in range(8):
            half[comp, big] = rows[comp, big, pl.ds(0, 8, 2), :] + rows[comp, big, pl.ds(1, 8, 2), :]
    return packed_pairs(half, 64)


def pack_body(
    initial_far, begin_far, end_far, x_low, x_high, y_low, y_high, opening,
    rows, half, initial, begin, end, arrived
):
    copies = [
        pltpu.make_async_copy(far.at[c], near.at[c], arrived.at[n, c])
        for n, (far, near) in enumerate(
            ((begin_far, begin), (end_far, end), (initial_far, initial))
        )
        for c in range(4)
    ]
    for copy in copies:
        copy.start()
    for copy in copies[:8]:
        copy.wait()
    for f in range(8):
        ref = begin if f < 4 else end
        x_low[f] = ref[f % 4, 0]
        x_high[f] = ref[f % 4, 15]
        for x in range(16):
            y_low[f, x : x + 1, :] = ref[f % 4, x, 0:1, :]
            y_high[f, x : x + 1, :] = ref[f % 4, x, 15:16, :]
    for copy in copies[8:]:
        copy.wait()
    packed = restricted_packed(initial, rows, half)
    for h in range(2):
        for x in range(4):
            opening[4 * h + x] = packed[h][16 * x : 16 * x + 16]
        x_low[8, 8 * h : 8 * h + 8] = packed[h][0:8]
        x_high[8, 8 * h : 8 * h + 8] = packed[h][56:64]
        for x in range(8):
            y_low[8, 8 * h + x : 8 * h + x + 1] = packed[h][8 * x : 8 * x + 1]
            y_high[8, 8 * h + x : 8 * h + x + 1] = packed[h][8 * x + 7 : 8 * x + 8]


def halves(pair):
    lane = index_along(pair.shape, 1)
    other = shifted(pair, 64, 1)
    return jnp.where(lane < 64, pair, other), jnp.where(lane < 64, other, pair)


def paired(low, high):
    return jnp.where(index_along(low.shape, 1) < 64, low, high)


def level2_pressure(r2, first, e2, step_z):
    r3 = [
        restricted_defect(
            r2[first + 2 * q + 1], r2[first + 2 * q + 2], r2[first + 2 * q + 3], r2[first + 2 * q + 4], 1, step_z
        )
        for q in range(16)
    ]
    p3 = deep_pressure(r3, 2, 2 * step_z)
    for i in range(8):
        e2[i] = r2[first + 14 + i] * (-16.0 / 9.0) + p3[i // 2]
    return [
        smoothed(e2[i], e2[i + 1], e2[i + 2], r2[first + 15 + i], 16.0, 1, step_z) for i in range(6)
    ]


def ordered(where, got, rows, base, size, blocks):
    own, partner, near, far, swapped = got
    k = where[1]
    blocks[4 + k, 0:size] = own[base : base + size]
    blocks[5 - k, 0:size] = partner[base : base + size]
    for j in range(2):
        low = rows * j + base
        turn = j * (2 * k - 1)
        blocks[3 + 3 * k + turn, 0:size] = near[low : low + size]
        blocks[1 + 7 * k + turn, 0:size] = far[low : low + size]
        blocks[6 - 3 * k - turn, 0:size] = swapped[low : low + size]
        blocks[8 - 7 * k - turn, 0:size] = swapped[2 * rows + low : 2 * rows + low + size]


def bit_lane(value, lane, step, bit):
    same = (lane // step) % 2 == bit
    return jnp.where(same, value, nxt(value, step, 1) if bit else prv(value, step, 1))


def fine_source_body(
    where, begin, end, left, right, low, high, old, opening, comb, out, comb0, rows, half, rim
):
    row = index_along((16, 128), 0)
    first, last = row == 0, row == 15

    def at(f, x):
        if x < 0:
            return left[f]
        if x > 15:
            return right[f]
        return (begin if f < 4 else end)[f % 4, x]

    def carried(f, x):
        base = f - f % 4
        here = at(f, x)
        grad_x = at(f, x + 1) - at(f, x - 1)
        above = jnp.where(last, high[f, x : x + 1, :], nxt(here, 1, 0))
        below = jnp.where(first, low[f, x : x + 1, :], prv(here, 1, 0))
        grad_z = nxt(here, 1, 1) - prv(here, 1, 1)
        return at(base, x) * grad_x + at(base + 1, x) * (above - below) + at(base + 2, x) * grad_z

    for x in range(16):
        for c in range(4):
            total = begin[c, x] - 0.125 * (carried(c, x) + carried(c + 4, x))
            if c == 2:
                total = total + 0.25 * (begin[3, x] + end[3, x])
            comb[c, x] = total
    out[0] = 0.5 * comb[0, 0]
    out[17] = -0.5 * comb[0, 15]
    for x in range(16):
        v = comb[1, x]
        w = comb[2, x]
        div = jnp.where(last, 0.0, nxt(v, 1, 0)) - jnp.where(first, 0.0, prv(v, 1, 0))
        div = div + nxt(w, 1, 1) - prv(w, 1, 1)
        if x < 15:
            div = div + comb[0, x + 1]
        if x > 0:
            div = div - comb[0, x - 1]
        out[x + 1] = 0.5 * div
        out[18, x : x + 1, :] = 0.5 * v[0:1]
        out[19, x : x + 1, :] = -0.5 * v[15:16]
    coarse_source(opening, left, right, low, high, comb0, out, rim)
    packed = restricted_packed(comb, rows, half)
    for h in range(2):
        for x in range(4):
            for n in range(2):
                part = packed[h][16 * x + 8 * n : 16 * x + 8 * n + 8] - old[h, 2 * x + n]
                part = part + jnp.where(where[0] == 0, comb0[h, 2 * x + n], 0.0)
                out[23 + 4 * h + x, 8 * n : 8 * n + 8] = part


def coarse_source(opening, left, right, low, high, comb0, out, rim):
    row = index_along((8, 128), 0)

    def inside(x):
        rows = 8 * (x % 2)
        return [
            *halves(opening[x // 2, rows : rows + 8]),
            *halves(opening[4 + x // 2, rows : rows + 8]),
        ]

    def outside(ref):
        return [*halves(ref[8, 0:8]), *halves(ref[8, 8:16])]

    plane = {x: inside(x) for x in range(8)}
    plane[-1], plane[8] = outside(left), outside(right)
    under, over = outside(low), outside(high)
    comb = []
    for x in range(8):
        u, v, w, b = plane[x]
        fresh = []
        for c in range(4):
            here = plane[x][c]
            above = jnp.where(row == 7, over[c][x : x + 1], nxt(here, 1, 0))
            below = jnp.where(row == 0, under[c][x : x + 1], prv(here, 1, 0))
            moving = u * (plane[x + 1][c] - plane[x - 1][c]) + v * (above - below)
            moving = moving + w * (nxt(here, 1, 1) - prv(here, 1, 1))
            fresh.append(here - 0.125 * moving + (0.5 * b if c == 2 else 0.0))
        comb.append(fresh)
        comb0[0, x] = paired(fresh[0], fresh[1])
        comb0[1, x] = paired(fresh[2], fresh[3])
    source = [0.25 * comb[0][0]]
    for x in range(8):
        u, v, w, b = comb[x]
        div = jnp.where(row == 7, 0.0, nxt(v, 1, 0)) - jnp.where(row == 0, 0.0, prv(v, 1, 0))
        div = div + nxt(w, 1, 1) - prv(w, 1, 1)
        if x < 7:
            div = div + comb[x + 1][0]
        if x > 0:
            div = div - comb[x - 1][0]
        source.append(0.25 * div)
        rim[0, x : x + 1, :] = 0.25 * v[0:1]
        rim[1, x : x + 1, :] = -0.25 * v[7:8]
    source.append(-0.25 * comb[7][0])
    source += [rim[0], rim[1]]
    for i in range(6):
        out[20 + i // 2, 8 * (i % 2) : 8 * (i % 2) + 8] = paired(source[2 * i], source[2 * i + 1])


def fine_down_body(
    where, below, own, above, across,
    message, inner, outer, r0, coarse_r1, r1, r2, rim, coarse_r2
):
    blocks = (below, own, above, across)
    for b, ref in enumerate(blocks):
        r0[:, 16 * b : 16 * b + 16] = ref[0:18]
    for b, ref in enumerate(blocks):
        for i in range(6):
            pair = halves(ref[20 + i // 2, 8 * (i % 2) : 8 * (i % 2) + 8])
            for n in range(2):
                if i < 5:
                    coarse_r1[2 * i + n, 8 * b : 8 * b + 8] = pair[n]
                else:
                    rim[b, n] = pair[n]
    for b in range(4):
        for x in range(8):
            coarse_r1[x + 1, 8 * b + 7 : 8 * b + 8] += rim[(b + 1) % 4, 0, x : x + 1, :]
            coarse_r1[x + 1, 8 * b : 8 * b + 1] += rim[(b + 3) % 4, 1, x : x + 1, :]
    nothing = jnp.zeros((32, 128), F32)

    def at(x):
        return coarse_r1[x + 1] if -1 <= x < 9 else nothing

    for x in range(-1, 5):
        coarse_r2[x + 1] = restricted_defect(at(2 * x - 1), at(2 * x), at(2 * x + 1), at(2 * x + 2), 1, 1)
    for b in range(4):
        upper, lower = blocks[(b + 1) % 4], blocks[(b + 3) % 4]
        for x in range(16):
            r0[x + 1, 16 * b + 15 : 16 * b + 16] += upper[18, x : x + 1, :]
            r0[x + 1, 16 * b : 16 * b + 1] += lower[19, x : x + 1, :]
    zero = jnp.zeros((64, 128), F32)

    def at0(x):
        return r0[x + 1] if -1 <= x < 17 else zero

    def at1(x):
        return r1[x + 1] if -1 <= x < 9 else zero

    for x in range(-1, 9):
        r1[x + 1] = restricted_defect(at0(2 * x - 1), at0(2 * x), at0(2 * x + 1), at0(2 * x + 2), 1, 1)
    for x in range(-1, 5):
        r2[x + 1] = restricted_defect(at1(2 * x - 1), at1(2 * x), at1(2 * x + 1), at1(2 * x + 2), 2, 2)
    lane = index_along((16, 128), 1)
    part = [r2[i, pl.ds(0, 16, 4), :] for i in range(6)]
    odd = lane % 2 == 1
    first = jnp.where(
        lane % 4 < 2, jnp.where(odd, part[1], part[0]), jnp.where(odd, part[3], part[2])
    )
    second = jnp.where(odd, part[5], part[4])
    message[0:16] = first
    message[16:32] = second
    part = [coarse_r2[i, pl.ds(0, 16, 2), :] for i in range(6)]
    message[32:48] = paired(jnp.where(odd, part[1], part[0]), jnp.where(odd, part[3], part[2]))
    message[48:64] = jnp.where(odd, part[5], part[4])
    k = where[1]
    for i in range(3):
        inner[384 + 32 * i : 416 + 32 * i] = coarse_r1[7 - 7 * k + i]
        outer[384 + 32 * i : 416 + 32 * i] = coarse_r1[7 * k + i]
    for i in range(6):
        inner[64 * i : 64 * i + 64] = r0[12 - 12 * k + i]
        outer[64 * i : 64 * i + 64] = r0[12 * k + i]


def sum_parts(parts, r2):
    for j in range(10):
        for n in range(4):
            value = parts[j][n + 1]
            if n == 0 and j > 0:
                value = value + parts[j - 1][5]
            if n == 3 and j < 9:
                value = value + parts[j + 1][0]
            r2[4 * j + n] = value


def fine_up_body(
    where, own, partner, near, far, swapped, face_in, face_out, mine, comb, below, own_share, above, across_jump, fine, jump,
    r0, r1, r2, e2, p2, e1, p1, e0, p0, rows, half, blocks
):
    k = where[1]
    ordered(where, (own, partner, near, far, swapped), 64, 0, 32, blocks)
    r0[5:21] = mine[1:17]
    for i in range(6):
        inside = face_in[64 * i : 64 * i + 64]
        outside = face_out[64 * i : 64 * i + 64]
        left = jnp.where(k == 0, outside, inside)
        right = jnp.where(k == 0, inside, outside)
        if i < 5:
            r0[i] = left
        else:
            r0[5] += left
        if i > 0:
            r0[20 + i] = right
        else:
            r0[20] += right
    r0[4] += mine[0]
    r0[21] += mine[17]
    lane = index_along((16, 128), 1)
    parts = []
    for j in range(10):
        first, second = blocks[j, 0:16], blocks[j, 16:32]
        even, odd = bit_lane(first, lane, 2, 0), bit_lane(first, lane, 2, 1)
        parts.append(
            [
                bit_lane(even, lane, 1, 0),
                bit_lane(even, lane, 1, 1),
                bit_lane(odd, lane, 1, 0),
                bit_lane(odd, lane, 1, 1),
                bit_lane(second, lane, 1, 0),
                bit_lane(second, lane, 1, 1),
            ]
        )
    sum_parts(parts, r2)
    for i, value in enumerate(level2_pressure(r2, 4 * k, e2, 4)):
        for y2 in range(16):
            p2[i, 4 * y2 : 4 * y2 + 4, :] = jnp.broadcast_to(value[y2 : y2 + 1], (4, 128))
    for k in range(12):
        a = 2 * k + 1
        r1[k] = restricted_defect(r0[a - 1], r0[a], r0[a + 1], r0[a + 2], 1, 1)
        e1[k] = r1[k] * (-4.0 / 9.0) + p2[k // 2]
    for k in range(10):
        p1[k] = smoothed(e1[k], e1[k + 1], e1[k + 2], r1[k + 1], 4.0, 2, 2)
    for j in range(20):
        e0[j] = r0[j + 3] * (-1.0 / 9.0) + p1[j // 2]
    for j in range(18):
        p0[j] = smoothed(e0[j], e0[j + 1], e0[j + 2], r0[j + 4], 1.0, 1, 1)
    for big in range(8):
        a = 2 * big + 1
        pair = p0[a] + p0[a + 1]
        rows[0, big] = p0[a + 1] + p0[a + 2] - p0[a - 1] - p0[a]
        rows[1, big] = nxt(pair, 1, 0) - prv(pair, 1, 0)
        rows[2, big] = nxt(pair, 1, 1) - prv(pair, 1, 1)
    for c in range(3):
        for big in range(8):
            half[c, big] = rows[c, big, pl.ds(0, 32, 2), :] + rows[c, big, pl.ds(1, 32, 2), :]
    packed = packed_pairs(half, 256)
    for h in range(2):
        slope = 0.5 * packed[h].reshape(8, 32, 128)
        for b, (ref, first) in enumerate(((below, 23), (own_share, 23), (above, 23), (across_jump, 0))):
            for x in range(8):
                jump[h, x, 8 * b : 8 * b + 8] = (
                    ref[first + 4 * h + x // 2, 8 * (x % 2) : 8 * (x % 2) + 8]
                    - slope[x, 8 * b : 8 * b + 8]
                )
    for x in range(16):
        here = p0[x + 1, 8:40]
        fine[0, x] = comb[0, x] - 0.5 * (p0[x + 2, 16:32] - p0[x, 16:32])
        fine[1, x] = comb[1, x] - 0.5 * (nxt(here, 1, 0) - prv(here, 1, 0))[8:24]
        mid = here[8:24]
        fine[2, x] = comb[2, x] - 0.5 * (nxt(mid, 1, 1) - prv(mid, 1, 1))
        fine[3, x] = comb[3, x]


def coarse_down_body(before, low, high, after, comb_out, r1, message, state, comb, r2):
    lane = index_along((32, 128), 1)
    for side, ref in enumerate((before, low, high, after)):
        for x in range(4):
            for h in range(2):
                pair = ref[h, x]
                other = shifted(pair, 64, 1)
                state[2 * h, 4 * side + x] = jnp.where(lane < 64, pair, other)
                state[2 * h + 1, 4 * side + x] = jnp.where(lane < 64, other, pair)
    message[...] = coarse_down_core(comb_out, r1, state, comb, r2)


def coarse_down_core(comb_out, r1, state, comb, r2):
    for i in range(1, 15):
        for c in range(3):
            total = state[c, i] - 0.125 * advected(state, i, c)
            if c == 2:
                total = total + 0.5 * state[3, i]
            comb[c, i - 1] = total
            if 4 <= i < 12:
                comb_out[c, i - 4] = total
    for x in range(8):
        comb_out[3, x] = state[3, x + 4] - 0.125 * advected(state, x + 4, 3)
    for k in range(12):
        v = comb[1, k + 1]
        w = comb[2, k + 1]
        div = comb[0, k + 2] - comb[0, k] + nxt(v, 1, 0) - prv(v, 1, 0) + nxt(w, 1, 1) - prv(w, 1, 1)
        r1[k] = 0.25 * div
    for m in range(4):
        a = 2 * m + 2
        r2[m] = restricted_defect(r1[a - 1], r1[a], r1[a + 1], r1[a + 2], 1, 1)
    part = [r2[m, pl.ds(0, 16, 2), :] for m in range(4)]
    lane = index_along((16, 128), 1)
    odd = lane % 2 == 1
    return jnp.where(
        lane < 64, jnp.where(odd, part[1], part[0]), jnp.where(odd, part[3], part[2])
    )


def coarse_up_core(where, got, comb, r1, blocks, r2, e2, p2, e1, p1, emit):
    ordered(where, got, 16, 0, 16, blocks)
    lane = index_along((16, 128), 1)
    for j in range(10):
        for m, pair in enumerate(halves(blocks[j])):
            r2[4 * j + 2 * m] = bit_lane(pair, lane, 1, 0)
            r2[4 * j + 2 * m + 1] = bit_lane(pair, lane, 1, 1)
    level1_pressure(where, r1, r2, e2, p2, e1, p1)
    for x in range(8):
        u, v, w = slopes(p1, x)
        emit(0, x, paired(comb[0, x] - u, comb[1, x] - v))
        emit(1, x, paired(comb[2, x] - w, comb[3, x]))


def level1_pressure(where, r1, r2, e2, p2, e1, p1):
    for i, value in enumerate(level2_pressure(r2, 4 * where[1], e2, 2)):
        p2[i, pl.ds(0, 16, 2), :] = value
        p2[i, pl.ds(1, 16, 2), :] = value
    for k in range(12):
        e1[k] = r1[k] * (-4.0 / 9.0) + p2[k // 2]
    for k in range(10):
        p1[k] = smoothed(e1[k], e1[k + 1], e1[k + 2], r1[k + 1], 4.0, 1, 1)


def slopes(p1, x):
    here = p1[x + 1]
    return (
        0.25 * (p1[x + 2] - p1[x]),
        0.25 * (nxt(here, 1, 0) - prv(here, 1, 0)),
        0.25 * (nxt(here, 1, 1) - prv(here, 1, 1)),
    )


UP_SCRATCH = [(10, 16, 128), (40, 16, 128), (8, 16, 128), (6, 32, 128), (12, 32, 128), (10, 32, 128)]


def coarse_up_first_body(
    where, own, partner, near, far, swapped, face_in, face_out, mine, comb0, jump,
    ended, after, low, high, blocks, r2, e2, p2, e1, p1, r1
):
    k = where[1]
    ordered(where, (own, partner, near, far, swapped), 64, 32, 32, blocks)
    lane = index_along((16, 128), 1)
    parts = []
    for j in range(10):
        second = blocks[j, 16:32]
        shares = []
        for pair in halves(blocks[j, 0:16]):
            shares += [bit_lane(pair, lane, 1, 0), bit_lane(pair, lane, 1, 1)]
        parts.append(shares + [bit_lane(second, lane, 1, 0), bit_lane(second, lane, 1, 1)])
    sum_parts(parts, r2)
    r1[2:10] = mine[1:9]
    for i in range(3):
        inside = face_in[384 + 32 * i : 416 + 32 * i]
        outside = face_out[384 + 32 * i : 416 + 32 * i]
        left = jnp.where(k == 0, outside, inside)
        right = jnp.where(k == 0, inside, outside)
        if i < 2:
            r1[i] = left
        else:
            r1[2] += left
        if i > 0:
            r1[9 + i] = right
        else:
            r1[9] += right
    r1[1] += mine[0]
    r1[10] += mine[9]
    level1_pressure(where, r1, r2, e2, p2, e1, p1)
    for x in range(8):
        u, v, w = slopes(p1, x)
        for h, change in enumerate((paired(u, v), paired(w, jnp.zeros_like(w)))):
            value = jump[h, x] - change
            ref = low if x < 4 else high
            ref[h, x % 4] = value
            after[h, x] = value[8:16]
            ended[h, x] = comb0[h, x] - change[8:16]


def coarse_up_middle_body(where, a, b, c, d, e, comb, r1, jump, ended, own, low, high, *scratch):
    def emit(h, x, value):
        after = value + jump[h, x]
        ref = low if x < 4 else high
        ref[h, x % 4] = after
        ended[h, x] = value[8:16]
        own[h, x] = after[8:16]

    coarse_up_core(where, (a, b, c, d, e), comb, r1, *scratch, emit)


def coarse_up_last_body(where, a, b, c, d, e, comb, r1, ended, *scratch):
    def emit(h, x, value):
        ended[h, x] = value[8:16]

    coarse_up_core(where, (a, b, c, d, e), comb, r1, *scratch, emit)


def new_start_body(where, fine, initial, state, out, rows, half, tall):
    t = where[0]

    @pl.when(t == 0)
    def _():
        out[...] = initial[...]

    @pl.when(t > 0)
    def _():
        packed = restricted_packed(fine, rows, half)
        for h in range(2):
            change = state[h].reshape(64, 128) - packed[h]
            for side in range(2):
                comp = 2 * h + side
                wide = dot(change, z_spread(side)).reshape(8, 8, 128)
                for x in range(8):
                    tall[comp, x, pl.ds(0, 8, 2), :] = wide[x]
                    tall[comp, x, pl.ds(1, 8, 2), :] = wide[x]
        for comp in range(4):
            for x in range(16):
                out[comp, x] = fine[comp, x] + tall[comp, x // 2]


def coarse_end_body(where, e0, e1, e2, e3, out):
    t = where[0]
    for h in range(2):
        low = jnp.where(t == 0, e0[h], e1[h])
        high = jnp.where(t == 2, e2[h], e3[h])
        value = jnp.where(t < 2, low, high)
        out[2 * h] = value[:, :, :64]
        out[2 * h + 1] = shifted(value, 64, 2)[:, :, :64]


def moved(value, axis, step):
    count = lax.axis_size(axis)
    return lax.ppermute(value, axis, [(i, (i + step) % count) for i in range(count)])


def both_sides(low_face, high_face, axis, step=1):
    return moved(high_face, axis, step), moved(low_face, axis, -step)


def around(value, axis):
    return [moved(value, axis, step) for step in range(1, 4)]


def swapped_cores(value):
    return lax.ppermute(value, "sx", [(i, i ^ 1) for i in range(lax.axis_size("sx"))])


def from_chips(value, chips):
    count = lax.axis_size("sx")
    far = 2 * chips - 1
    return lax.ppermute(
        value, "sx", [(i, (i + (far if i % 2 else -far)) % count) for i in range(count)]
    )


def five_chips(message):
    partner = swapped_cores(message)
    both = jnp.concatenate([message, partner], axis=0)
    near, far = from_chips(both, 1), from_chips(both, 2)
    return [message, partner, near, far, swapped_cores(jnp.concatenate([near, far], axis=0))]


def sent(value, source, target):
    return lax.ppermute(value, "tm", [(source, target)])


def shards(initial_state, start_old, end_old, coarse_old):
    begin, end, old = start_old[0], end_old[0], coarse_old[0]
    where = jnp.stack([lax.axis_index("tm"), lax.axis_index("sx") % 2]).astype(jnp.int32)

    x_low, x_high, y_low, y_high, opening = call(
        pack_body,
        [(9, 16, 128)] * 4 + [(8, 16, 128)],
        [initial_state, begin, end],
        [(4, 8, 16, 128), (4, 8, 8, 128)] + [(4, 16, 16, 128)] * 3,
        limit=56,
        far=True,
    )
    old_packed = jnp.stack(
        [jnp.concatenate([old[0], old[1]], axis=-1), jnp.concatenate([old[2], old[3]], axis=-1)]
    )
    left, right = both_sides(x_low, x_high, "sx")
    low, high = both_sides(y_low, y_high, "sy")
    comb, share, comb0 = call(
        fine_source_body,
        [(4, 16, 16, 128), (31, 16, 128), (2, 8, 8, 128)],
        [where, begin, end, left, right, low, high, old_packed, opening],
        [(4, 8, 16, 128), (4, 8, 8, 128), (2, 8, 128)],
        smem=1,
    )
    below, above = both_sides(share, share, "sy")
    across = moved(share[:23], "sy", 2)

    def coarse_down(state):
        low, high = state
        before, after = both_sides(low, high, "sx")
        return call(
            coarse_down_body,
            [(4, 8, 32, 128), (12, 32, 128), (16, 128)],
            [before, low, high, after],
            [(4, 16, 32, 128), (3, 14, 32, 128), (4, 32, 128)],
        )

    message, inner, outer, r0, first0 = call(
        fine_down_body,
        [(64, 128), (480, 128), (480, 128), (18, 64, 128), (10, 32, 128)],
        [where, below, share, above, across],
        [(10, 64, 128), (6, 64, 128), (4, 2, 8, 128), (6, 32, 128)],
        smem=1,
    )
    across_jump = moved(share[23:], "sy", 2)
    partner = swapped_cores(jnp.concatenate([message, inner], axis=0))
    both = jnp.concatenate([message, partner[:64]], axis=0)
    near, far = from_chips(jnp.concatenate([both, outer], axis=0), 1), from_chips(both, 2)
    near, far, across_jump = lax.optimization_barrier((near, far, across_jump))
    crossed = swapped_cores(jnp.concatenate([near[:128], far], axis=0))
    got = [message, partner, near, far, crossed]
    fine_end, jump0 = call(
        fine_up_body,
        [(4, 16, 16, 128), (2, 8, 32, 128)],
        [where] + got + [partner[64:], near[128:], r0, comb, below, share, above, across_jump],
        [
            (26, 64, 128),
            (12, 64, 128),
            (40, 16, 128),
            (8, 16, 128),
            (6, 64, 128),
            (12, 64, 128),
            (10, 64, 128),
            (20, 64, 128),
            (18, 64, 128),
            (3, 8, 64, 128),
            (3, 8, 32, 128),
            (10, 32, 128),
        ],
        smem=1,
    )

    def coarse_up(body, args, scratch):
        ended, own, low, high = call(
            body,
            [(2, 8, 8, 128)] * 2 + [(2, 4, 32, 128)] * 2,
            [where] + args,
            scratch,
            smem=1,
        )
        return ended, own, [low, high]

    ended0, own1, c1 = coarse_up(
        coarse_up_first_body,
        got + [partner[64:], near[128:], first0, comb0, jump0],
        [(10, 32, 128)] + UP_SCRATCH[1:] + [(12, 32, 128)],
    )
    jump1 = lax.ppermute(jump0, "tm", [(1, 0), (2, 1)])
    fine_before = moved(fine_end, "tm", 1)

    combined, level1, message = coarse_down(c1)
    got, jump1 = lax.optimization_barrier((five_chips(message), jump1))
    ended1, own2, c2 = coarse_up(coarse_up_middle_body, got + [combined, level1, jump1], UP_SCRATCH)

    combined, level1, message = coarse_down(c2)
    jump2 = sent(jump1, 1, 0)
    hand1 = sent(jnp.concatenate([own1, ended1], axis=0), 0, 1)
    got, hand1, jump2, fine_before = lax.optimization_barrier(
        (five_chips(message), hand1, jump2, fine_before)
    )
    ended2, own3, c3 = coarse_up(coarse_up_middle_body, got + [combined, level1, jump2], UP_SCRATCH)

    combined, level1, message = coarse_down(c3)
    hand2 = sent(jnp.concatenate([own2, ended2], axis=0), 0, 2)
    hand3 = sent(own3, 0, 3)
    got, hand2, hand3 = lax.optimization_barrier((five_chips(message), hand2, hand3))
    ended3 = call(
        coarse_up_last_body,
        (2, 8, 8, 128),
        [where] + got + [combined, level1],
        UP_SCRATCH,
        smem=1,
    )
    new_start = call(
        new_start_body,
        (4, 16, 16, 128),
        [where, fine_before, initial_state, hand1[:2] + hand2[:2] + hand3],
        [(4, 8, 16, 128), (4, 8, 8, 128), (4, 8, 16, 128)],
        smem=1,
    )
    coarse_end = call(
        coarse_end_body,
        (4, 8, 8, 64),
        [where, ended0, hand1[2:], hand2[2:], sent(ended3, 0, 3)],
        smem=1,
    )
    return (new_start[None], fine_end[None], coarse_end[None])


def solution(mesh):
    in_specs = (
        P(None, "sx", "sy", None),
        P("tm", None, "sx", "sy", None),
        P("tm", None, "sx", "sy", None),
        P("tm", None, "sx", "sy", None),
    )
    out_specs = (
        P("tm", None, "sx", "sy", None),
        P("tm", None, "sx", "sy", None),
        P("tm", None, "sx", "sy", None),
    )
    return jax.shard_map(shards, mesh=mesh, in_specs=in_specs, out_specs=out_specs, check_vma=False)
```

```python
import jax
import jax.numpy as jnp
from jax import lax
from jax.experimental import pallas as pl
from jax.experimental.pallas import tpu as pltpu
from jax.sharding import PartitionSpec as P

F32 = jnp.float32
HIGH = lax.Precision.HIGHEST


def call(body, outs, args, scratch=(), smem=0, limit=24, far=False):
    vmem = pl.BlockSpec(memory_space=pltpu.VMEM)
    scalar = pl.BlockSpec(memory_space=pltpu.SMEM)
    single = not isinstance(outs, list)
    shapes = [outs] if single else outs
    got = pl.pallas_call(
        body,
        out_shape=[jax.ShapeDtypeStruct(s, F32) for s in shapes],
        in_specs=[scalar] * smem
        + [pl.BlockSpec(memory_space=pl.ANY) if far else vmem] * (len(args) - smem),
        out_specs=[vmem] * len(shapes),
        scratch_shapes=[pltpu.VMEM(s, F32) for s in scratch]
        + ([pltpu.SemaphoreType.DMA((3, 4))] if far else []),
        compiler_params=pltpu.CompilerParams(vmem_limit_bytes=limit * 2**20),
        name=body.__name__,
    )(*args)
    return got[0] if single else got


def shifted(value, amount, axis):
    return pltpu.roll(value, amount % value.shape[axis], axis)


def nxt(value, step, axis):
    return shifted(value, -step, axis)


def prv(value, step, axis):
    return shifted(value, step, axis)


def index_along(shape, axis):
    return lax.broadcasted_iota(jnp.int32, shape, axis)


def pair_sum(value, step, axis):
    upper = (index_along(value.shape, axis) // step) % 2 == 1
    return value + jnp.where(upper, prv(value, step, axis), nxt(value, step, axis))


def ring_sum(value, step_y, step_z):
    return (
        nxt(value, step_y, 0)
        + prv(value, step_y, 0)
        + nxt(value, step_z, 1)
        + prv(value, step_z, 1)
    )


def restricted_defect(before, first, second, after, step_y, step_z):
    both = first + second
    total = both * (1.0 / 3.0) + (before + both + after + ring_sum(both, step_y, step_z)) * (1.0 / 9.0)
    return pair_sum(pair_sum(total, step_y, 0), step_z, 1) * 0.125


def smoothed(before, here, after, source, spacing_sq, step_y, step_z):
    around = before + after + ring_sum(here, step_y, step_z)
    return here * (1.0 / 3.0) + (around - spacing_sq * source) * (1.0 / 9.0)


def deep_pressure(r3, step_y, step_z):
    r4 = [
        restricted_defect(r3[2 * w], r3[2 * w + 1], r3[2 * w + 2], r3[2 * w + 3], step_y, step_z)
        for w in range(7)
    ]
    low_y, low_z = 2 * step_y, 2 * step_z
    p4 = [r * (-256.0 / 9.0) for r in r4]
    for sweep in range(2):
        inner = range(1 + sweep, 6 - sweep)
        fresh = {w: smoothed(p4[w - 1], p4[w], p4[w + 1], r4[w], 256.0, low_y, low_z) for w in inner}
        p4 = [fresh.get(w) for w in range(7)]
    e3 = {q: r3[q] * (-64.0 / 9.0) + p4[(q - 7) // 2 + 3] for q in range(5, 11)}
    return [
        smoothed(e3[q - 1], e3[q], e3[q + 1], r3[q], 64.0, step_y, step_z) for q in range(6, 10)
    ]


def advected(ref, i, comp):
    here = ref[comp, i]
    grad_x = ref[comp, i + 1] - ref[comp, i - 1]
    grad_y = nxt(here, 1, 0) - prv(here, 1, 0)
    grad_z = nxt(here, 1, 1) - prv(here, 1, 1)
    return ref[0, i] * grad_x + ref[1, i] * grad_y + ref[2, i] * grad_z


def z_pick(high):
    k = index_along((128, 128), 0)
    j = index_along((128, 128), 1)
    return jnp.where(k // 2 == j - 64 * high, 1.0, 0.0).astype(F32)


def z_spread(high):
    k = index_along((128, 128), 0)
    j = index_along((128, 128), 1)
    return jnp.where(k == j // 2 + 64 * high, 1.0, 0.0).astype(F32)


def dot(a, b):
    return lax.dot_general(a, b, (((1,), (0,)), ((), ())), precision=HIGH, preferred_element_type=F32)


def packed_pairs(half, rows):
    low, high = z_pick(0), z_pick(1)
    packed = []
    for h in range(2):
        value = dot(half[2 * h].reshape(rows, 128), low)
        if 2 * h + 1 < half.shape[0]:
            value = value + dot(half[2 * h + 1].reshape(rows, 128), high)
        packed.append(0.125 * value)
    return packed


def restricted_packed(fine, rows, half):
    for comp in range(4):
        for big in range(8):
            rows[comp, big] = fine[comp, 2 * big] + fine[comp, 2 * big + 1]
    for comp in range(4):
        for big in range(8):
            half[comp, big] = rows[comp, big, pl.ds(0, 8, 2), :] + rows[comp, big, pl.ds(1, 8, 2), :]
    return packed_pairs(half, 64)


def pack_body(
    initial_far, begin_far, end_far, x_low, x_high, y_low, y_high, opening,
    rows, half, initial, begin, end, arrived
):
    copies = [
        pltpu.make_async_copy(far.at[c], near.at[c], arrived.at[n, c])
        for n, (far, near) in enumerate(
            ((begin_far, begin), (end_far, end), (initial_far, initial))
        )
        for c in range(4)
    ]
    for copy in copies:
        copy.start()
    for copy in copies[:8]:
        copy.wait()
    for f in range(8):
        ref = begin if f < 4 else end
        x_low[f] = ref[f % 4, 0]
        x_high[f] = ref[f % 4, 15]
        for x in range(16):
            y_low[f, x : x + 1, :] = ref[f % 4, x, 0:1, :]
            y_high[f, x : x + 1, :] = ref[f % 4, x, 15:16, :]
    for copy in copies[8:]:
        copy.wait()
    packed = restricted_packed(initial, rows, half)
    for h in range(2):
        for x in range(4):
            opening[4 * h + x] = packed[h][16 * x : 16 * x + 16]
        x_low[8, 8 * h : 8 * h + 8] = packed[h][0:8]
        x_high[8, 8 * h : 8 * h + 8] = packed[h][56:64]
        for x in range(8):
            y_low[8, 8 * h + x : 8 * h + x + 1] = packed[h][8 * x : 8 * x + 1]
            y_high[8, 8 * h + x : 8 * h + x + 1] = packed[h][8 * x + 7 : 8 * x + 8]


def halves(pair):
    lane = index_along(pair.shape, 1)
    other = shifted(pair, 64, 1)
    return jnp.where(lane < 64, pair, other), jnp.where(lane < 64, other, pair)


def paired(low, high):
    return jnp.where(index_along(low.shape, 1) < 64, low, high)


def level2_pressure(r2, first, e2, step_z):
    r3 = [
        restricted_defect(
            r2[first + 2 * q + 1], r2[first + 2 * q + 2], r2[first + 2 * q + 3], r2[first + 2 * q + 4], 1, step_z
        )
        for q in range(16)
    ]
    p3 = deep_pressure(r3, 2, 2 * step_z)
    for i in range(8):
        e2[i] = r2[first + 14 + i] * (-16.0 / 9.0) + p3[i // 2]
    return [
        smoothed(e2[i], e2[i + 1], e2[i + 2], r2[first + 15 + i], 16.0, 1, step_z) for i in range(6)
    ]


def ordered(where, got, rows, base, size, blocks):
    own, partner, near, far, swapped = got
    k = where[1]
    blocks[4 + k, 0:size] = own[base : base + size]
    blocks[5 - k, 0:size] = partner[base : base + size]
    for j in range(2):
        low = rows * j + base
        turn = j * (2 * k - 1)
        blocks[3 + 3 * k + turn, 0:size] = near[low : low + size]
        blocks[1 + 7 * k + turn, 0:size] = far[low : low + size]
        blocks[6 - 3 * k - turn, 0:size] = swapped[low : low + size]
        blocks[8 - 7 * k - turn, 0:size] = swapped[2 * rows + low : 2 * rows + low + size]


def bit_lane(value, lane, step, bit):
    same = (lane // step) % 2 == bit
    return jnp.where(same, value, nxt(value, step, 1) if bit else prv(value, step, 1))


def fine_source_body(
    where, begin, end, left, right, low, high, old, opening, comb, out, comb0, rows, half, rim
):
    row = index_along((16, 128), 0)
    first, last = row == 0, row == 15

    def at(f, x):
        if x < 0:
            return left[f]
        if x > 15:
            return right[f]
        return (begin if f < 4 else end)[f % 4, x]

    def carried(f, x):
        base = f - f % 4
        here = at(f, x)
        grad_x = at(f, x + 1) - at(f, x - 1)
        above = jnp.where(last, high[f, x : x + 1, :], nxt(here, 1, 0))
        below = jnp.where(first, low[f, x : x + 1, :], prv(here, 1, 0))
        grad_z = nxt(here, 1, 1) - prv(here, 1, 1)
        return at(base, x) * grad_x + at(base + 1, x) * (above - below) + at(base + 2, x) * grad_z

    for x in range(16):
        for c in range(4):
            total = begin[c, x] - 0.125 * (carried(c, x) + carried(c + 4, x))
            if c == 2:
                total = total + 0.25 * (begin[3, x] + end[3, x])
            comb[c, x] = total
    out[0] = 0.5 * comb[0, 0]
    out[17] = -0.5 * comb[0, 15]
    for x in range(16):
        v = comb[1, x]
        w = comb[2, x]
        div = jnp.where(last, 0.0, nxt(v, 1, 0)) - jnp.where(first, 0.0, prv(v, 1, 0))
        div = div + nxt(w, 1, 1) - prv(w, 1, 1)
        if x < 15:
            div = div + comb[0, x + 1]
        if x > 0:
            div = div - comb[0, x - 1]
        out[x + 1] = 0.5 * div
        out[18, x : x + 1, :] = 0.5 * v[0:1]
        out[19, x : x + 1, :] = -0.5 * v[15:16]
    coarse_source(opening, left, right, low, high, comb0, out, rim)
    packed = restricted_packed(comb, rows, half)
    for h in range(2):
        for x in range(4):
            for n in range(2):
                part = packed[h][16 * x + 8 * n : 16 * x + 8 * n + 8] - old[h, 2 * x + n]
                part = part + jnp.where(where[0] == 0, comb0[h, 2 * x + n], 0.0)
                out[23 + 4 * h + x, 8 * n : 8 * n + 8] = part


def coarse_source(opening, left, right, low, high, comb0, out, rim):
    row = index_along((8, 128), 0)

    def inside(x):
        rows = 8 * (x % 2)
        return [
            *halves(opening[x // 2, rows : rows + 8]),
            *halves(opening[4 + x // 2, rows : rows + 8]),
        ]

    def outside(ref):
        return [*halves(ref[8, 0:8]), *halves(ref[8, 8:16])]

    plane = {x: inside(x) for x in range(8)}
    plane[-1], plane[8] = outside(left), outside(right)
    under, over = outside(low), outside(high)
    comb = []
    for x in range(8):
        u, v, w, b = plane[x]
        fresh = []
        for c in range(4):
            here = plane[x][c]
            above = jnp.where(row == 7, over[c][x : x + 1], nxt(here, 1, 0))
            below = jnp.where(row == 0, under[c][x : x + 1], prv(here, 1, 0))
            moving = u * (plane[x + 1][c] - plane[x - 1][c]) + v * (above - below)
            moving = moving + w * (nxt(here, 1, 1) - prv(here, 1, 1))
            fresh.append(here - 0.125 * moving + (0.5 * b if c == 2 else 0.0))
        comb.append(fresh)
        comb0[0, x] = paired(fresh[0], fresh[1])
        comb0[1, x] = paired(fresh[2], fresh[3])
    source = [0.25 * comb[0][0]]
    for x in range(8):
        u, v, w, b = comb[x]
        div = jnp.where(row == 7, 0.0, nxt(v, 1, 0)) - jnp.where(row == 0, 0.0, prv(v, 1, 0))
        div = div + nxt(w, 1, 1) - prv(w, 1, 1)
        if x < 7:
            div = div + comb[x + 1][0]
        if x > 0:
            div = div - comb[x - 1][0]
        source.append(0.25 * div)
        rim[0, x : x + 1, :] = 0.25 * v[0:1]
        rim[1, x : x + 1, :] = -0.25 * v[7:8]
    source.append(-0.25 * comb[7][0])
    source += [rim[0], rim[1]]
    for i in range(6):
        out[20 + i // 2, 8 * (i % 2) : 8 * (i % 2) + 8] = paired(source[2 * i], source[2 * i + 1])


def fine_down_body(
    where, below, own, above, across,
    message, inner, outer, r0, coarse_r1, r1, r2, rim, coarse_r2
):
    blocks = (below, own, above, across)
    for b, ref in enumerate(blocks):
        r0[:, 16 * b : 16 * b + 16] = ref[0:18]
    for b, ref in enumerate(blocks):
        for i in range(6):
            pair = halves(ref[20 + i // 2, 8 * (i % 2) : 8 * (i % 2) + 8])
            for n in range(2):
                if i < 5:
                    coarse_r1[2 * i + n, 8 * b : 8 * b + 8] = pair[n]
                else:
                    rim[b, n] = pair[n]
    for b in range(4):
        for x in range(8):
            coarse_r1[x + 1, 8 * b + 7 : 8 * b + 8] += rim[(b + 1) % 4, 0, x : x + 1, :]
            coarse_r1[x + 1, 8 * b : 8 * b + 1] += rim[(b + 3) % 4, 1, x : x + 1, :]
    nothing = jnp.zeros((32, 128), F32)

    def at(x):
        return coarse_r1[x + 1] if -1 <= x < 9 else nothing

    for x in range(-1, 5):
        coarse_r2[x + 1] = restricted_defect(at(2 * x - 1), at(2 * x), at(2 * x + 1), at(2 * x + 2), 1, 1)
    for b in range(4):
        upper, lower = blocks[(b + 1) % 4], blocks[(b + 3) % 4]
        for x in range(16):
            r0[x + 1, 16 * b + 15 : 16 * b + 16] += upper[18, x : x + 1, :]
            r0[x + 1, 16 * b : 16 * b + 1] += lower[19, x : x + 1, :]
    zero = jnp.zeros((64, 128), F32)

    def at0(x):
        return r0[x + 1] if -1 <= x < 17 else zero

    def at1(x):
        return r1[x + 1] if -1 <= x < 9 else zero

    for x in range(-1, 9):
        r1[x + 1] = restricted_defect(at0(2 * x - 1), at0(2 * x), at0(2 * x + 1), at0(2 * x + 2), 1, 1)
    for x in range(-1, 5):
        r2[x + 1] = restricted_defect(at1(2 * x - 1), at1(2 * x), at1(2 * x + 1), at1(2 * x + 2), 2, 2)
    lane = index_along((16, 128), 1)
    part = [r2[i, pl.ds(0, 16, 4), :] for i in range(6)]
    odd = lane % 2 == 1
    first = jnp.where(
        lane % 4 < 2, jnp.where(odd, part[1], part[0]), jnp.where(odd, part[3], part[2])
    )
    second = jnp.where(odd, part[5], part[4])
    message[0:16] = first
    message[16:32] = second
    part = [coarse_r2[i, pl.ds(0, 16, 2), :] for i in range(6)]
    message[32:48] = paired(jnp.where(odd, part[1], part[0]), jnp.where(odd, part[3], part[2]))
    message[48:64] = jnp.where(odd, part[5], part[4])
    k = where[1]
    for i in range(3):
        inner[384 + 32 * i : 416 + 32 * i] = coarse_r1[7 - 7 * k + i]
        outer[384 + 32 * i : 416 + 32 * i] = coarse_r1[7 * k + i]
    for i in range(6):
        inner[64 * i : 64 * i + 64] = r0[12 - 12 * k + i]
        outer[64 * i : 64 * i + 64] = r0[12 * k + i]


def sum_parts(parts, r2):
    for j in range(10):
        for n in range(4):
            value = parts[j][n + 1]
            if n == 0 and j > 0:
                value = value + parts[j - 1][5]
            if n == 3 and j < 9:
                value = value + parts[j + 1][0]
            r2[4 * j + n] = value


def fine_up_body(
    where, own, partner, near, far, swapped, face_in, face_out, mine, below, own_share, above, across_jump, pressure, jump,
    r0, r1, r2, e2, p2, e1, p1, e0, p0, rows, half, blocks
):
    k = where[1]
    ordered(where, (own, partner, near, far, swapped), 64, 0, 32, blocks)
    r0[5:21] = mine[1:17]
    for i in range(6):
        inside = face_in[64 * i : 64 * i + 64]
        outside = face_out[64 * i : 64 * i + 64]
        left = jnp.where(k == 0, outside, inside)
        right = jnp.where(k == 0, inside, outside)
        if i < 5:
            r0[i] = left
        else:
            r0[5] += left
        if i > 0:
            r0[20 + i] = right
        else:
            r0[20] += right
    r0[4] += mine[0]
    r0[21] += mine[17]
    lane = index_along((16, 128), 1)
    parts = []
    for j in range(10):
        first, second = blocks[j, 0:16], blocks[j, 16:32]
        even, odd = bit_lane(first, lane, 2, 0), bit_lane(first, lane, 2, 1)
        parts.append(
            [
                bit_lane(even, lane, 1, 0),
                bit_lane(even, lane, 1, 1),
                bit_lane(odd, lane, 1, 0),
                bit_lane(odd, lane, 1, 1),
                bit_lane(second, lane, 1, 0),
                bit_lane(second, lane, 1, 1),
            ]
        )
    sum_parts(parts, r2)
    for i, value in enumerate(level2_pressure(r2, 4 * k, e2, 4)):
        for y2 in range(16):
            p2[i, 4 * y2 : 4 * y2 + 4, :] = jnp.broadcast_to(value[y2 : y2 + 1], (4, 128))
    for k in range(12):
        a = 2 * k + 1
        r1[k] = restricted_defect(r0[a - 1], r0[a], r0[a + 1], r0[a + 2], 1, 1)
        e1[k] = r1[k] * (-4.0 / 9.0) + p2[k // 2]
    for k in range(10):
        p1[k] = smoothed(e1[k], e1[k + 1], e1[k + 2], r1[k + 1], 4.0, 2, 2)
    for j in range(20):
        e0[j] = r0[j + 3] * (-1.0 / 9.0) + p1[j // 2]
    for j in range(18):
        p0[j] = smoothed(e0[j], e0[j + 1], e0[j + 2], r0[j + 4], 1.0, 1, 1)
    for big in range(8):
        a = 2 * big + 1
        pair = p0[a] + p0[a + 1]
        rows[0, big] = p0[a + 1] + p0[a + 2] - p0[a - 1] - p0[a]
        rows[1, big] = nxt(pair, 1, 0) - prv(pair, 1, 0)
        rows[2, big] = nxt(pair, 1, 1) - prv(pair, 1, 1)
    for c in range(3):
        for big in range(8):
            half[c, big] = rows[c, big, pl.ds(0, 32, 2), :] + rows[c, big, pl.ds(1, 32, 2), :]
    packed = packed_pairs(half, 256)
    for h in range(2):
        slope = 0.5 * packed[h].reshape(8, 32, 128)
        for b, (ref, first) in enumerate(((below, 23), (own_share, 23), (above, 23), (across_jump, 0))):
            for x in range(8):
                jump[h, x, 8 * b : 8 * b + 8] = (
                    ref[first + 4 * h + x // 2, 8 * (x % 2) : 8 * (x % 2) + 8]
                    - slope[x, 8 * b : 8 * b + 8]
                )
    pressure[...] = p0[:, 8:40]


def fine_end_body(pressure, comb, fine):
    for x in range(16):
        here = pressure[x + 1]
        mid = here[8:24]
        fine[0, x] = comb[0, x] - 0.5 * (pressure[x + 2, 8:24] - pressure[x, 8:24])
        fine[1, x] = comb[1, x] - 0.5 * (nxt(here, 1, 0) - prv(here, 1, 0))[8:24]
        fine[2, x] = comb[2, x] - 0.5 * (nxt(mid, 1, 1) - prv(mid, 1, 1))
        fine[3, x] = comb[3, x]


def coarse_down_body(where, inner, low, high, outer, comb_out, r1, message, state, comb, r2):
    lane = index_along((32, 128), 1)
    k = where[1]
    for side, ref in enumerate((outer, low, high, inner)):
        for x in range(4):
            for h in range(2):
                pair = ref[h, x]
                if side in (0, 3):
                    pair = jnp.where(k == 0, pair, (inner if side == 0 else outer)[h, x])
                other = shifted(pair, 64, 1)
                state[2 * h, 4 * side + x] = jnp.where(lane < 64, pair, other)
                state[2 * h + 1, 4 * side + x] = jnp.where(lane < 64, other, pair)
    message[...] = coarse_down_core(comb_out, r1, state, comb, r2)


def coarse_down_core(comb_out, r1, state, comb, r2):
    for i in range(1, 15):
        for c in range(3):
            total = state[c, i] - 0.125 * advected(state, i, c)
            if c == 2:
                total = total + 0.5 * state[3, i]
            comb[c, i - 1] = total
            if 4 <= i < 12:
                comb_out[c, i - 4] = total
    for x in range(8):
        comb_out[3, x] = state[3, x + 4] - 0.125 * advected(state, x + 4, 3)
    for k in range(12):
        v = comb[1, k + 1]
        w = comb[2, k + 1]
        div = comb[0, k + 2] - comb[0, k] + nxt(v, 1, 0) - prv(v, 1, 0) + nxt(w, 1, 1) - prv(w, 1, 1)
        r1[k] = 0.25 * div
    for m in range(4):
        a = 2 * m + 2
        r2[m] = restricted_defect(r1[a - 1], r1[a], r1[a + 1], r1[a + 2], 1, 1)
    part = [r2[m, pl.ds(0, 16, 2), :] for m in range(4)]
    lane = index_along((16, 128), 1)
    odd = lane % 2 == 1
    return jnp.where(
        lane < 64, jnp.where(odd, part[1], part[0]), jnp.where(odd, part[3], part[2])
    )


def coarse_up_core(where, got, comb, r1, blocks, r2, e2, p2, e1, p1, emit):
    ordered(where, got, 16, 0, 16, blocks)
    lane = index_along((16, 128), 1)
    for j in range(10):
        for m, pair in enumerate(halves(blocks[j])):
            r2[4 * j + 2 * m] = bit_lane(pair, lane, 1, 0)
            r2[4 * j + 2 * m + 1] = bit_lane(pair, lane, 1, 1)
    level1_pressure(where, r1, r2, e2, p2, e1, p1)
    for x in range(8):
        u, v, w = slopes(p1, x)
        emit(0, x, paired(comb[0, x] - u, comb[1, x] - v))
        emit(1, x, paired(comb[2, x] - w, comb[3, x]))


def level1_pressure(where, r1, r2, e2, p2, e1, p1):
    for i, value in enumerate(level2_pressure(r2, 4 * where[1], e2, 2)):
        p2[i, pl.ds(0, 16, 2), :] = value
        p2[i, pl.ds(1, 16, 2), :] = value
    for k in range(12):
        e1[k] = r1[k] * (-4.0 / 9.0) + p2[k // 2]
    for k in range(10):
        p1[k] = smoothed(e1[k], e1[k + 1], e1[k + 2], r1[k + 1], 4.0, 1, 1)


def slopes(p1, x):
    here = p1[x + 1]
    return (
        0.25 * (p1[x + 2] - p1[x]),
        0.25 * (nxt(here, 1, 0) - prv(here, 1, 0)),
        0.25 * (nxt(here, 1, 1) - prv(here, 1, 1)),
    )


UP_SCRATCH = [(10, 16, 128), (40, 16, 128), (8, 16, 128), (6, 32, 128), (12, 32, 128), (10, 32, 128)]


def coarse_up_first_body(
    where, own, partner, near, far, swapped, face_in, face_out, mine, comb0, jump,
    ended, after, low, high, blocks, r2, e2, p2, e1, p1, r1
):
    k = where[1]
    ordered(where, (own, partner, near, far, swapped), 64, 32, 32, blocks)
    lane = index_along((16, 128), 1)
    parts = []
    for j in range(10):
        second = blocks[j, 16:32]
        shares = []
        for pair in halves(blocks[j, 0:16]):
            shares += [bit_lane(pair, lane, 1, 0), bit_lane(pair, lane, 1, 1)]
        parts.append(shares + [bit_lane(second, lane, 1, 0), bit_lane(second, lane, 1, 1)])
    sum_parts(parts, r2)
    r1[2:10] = mine[1:9]
    for i in range(3):
        inside = face_in[384 + 32 * i : 416 + 32 * i]
        outside = face_out[384 + 32 * i : 416 + 32 * i]
        left = jnp.where(k == 0, outside, inside)
        right = jnp.where(k == 0, inside, outside)
        if i < 2:
            r1[i] = left
        else:
            r1[2] += left
        if i > 0:
            r1[9 + i] = right
        else:
            r1[9] += right
    r1[1] += mine[0]
    r1[10] += mine[9]
    level1_pressure(where, r1, r2, e2, p2, e1, p1)
    for x in range(8):
        u, v, w = slopes(p1, x)
        for h, change in enumerate((paired(u, v), paired(w, jnp.zeros_like(w)))):
            value = jump[h, x] - change
            ref = low if x < 4 else high
            ref[h, x % 4] = value
            after[h, x] = value[8:16]
            ended[h, x] = comb0[h, x] - change[8:16]


def coarse_up_middle_body(where, a, b, c, d, e, comb, r1, jump, ended, own, low, high, *scratch):
    def emit(h, x, value):
        after = value + jump[h, x]
        ref = low if x < 4 else high
        ref[h, x % 4] = after
        ended[h, x] = value[8:16]
        own[h, x] = after[8:16]

    coarse_up_core(where, (a, b, c, d, e), comb, r1, *scratch, emit)


def coarse_up_last_body(where, a, b, c, d, e, comb, r1, ended, *scratch):
    def emit(h, x, value):
        ended[h, x] = value[8:16]

    coarse_up_core(where, (a, b, c, d, e), comb, r1, *scratch, emit)


def new_start_body(where, fine, initial, state, out, rows, half, tall):
    t = where[0]

    @pl.when(t == 0)
    def _():
        out[...] = initial[...]

    @pl.when(t > 0)
    def _():
        packed = restricted_packed(fine, rows, half)
        for h in range(2):
            change = state[h].reshape(64, 128) - packed[h]
            for side in range(2):
                comp = 2 * h + side
                wide = dot(change, z_spread(side)).reshape(8, 8, 128)
                for x in range(8):
                    tall[comp, x, pl.ds(0, 8, 2), :] = wide[x]
                    tall[comp, x, pl.ds(1, 8, 2), :] = wide[x]
        for comp in range(4):
            for x in range(16):
                out[comp, x] = fine[comp, x] + tall[comp, x // 2]


def coarse_end_body(where, e0, e1, e2, e3, out):
    t = where[0]
    for h in range(2):
        low = jnp.where(t == 0, e0[h], e1[h])
        high = jnp.where(t == 2, e2[h], e3[h])
        value = jnp.where(t < 2, low, high)
        out[2 * h] = value[:, :, :64]
        out[2 * h + 1] = shifted(value, 64, 2)[:, :, :64]


def moved(value, axis, step):
    count = lax.axis_size(axis)
    return lax.ppermute(value, axis, [(i, (i + step) % count) for i in range(count)])


def both_sides(low_face, high_face, axis, step=1):
    return moved(high_face, axis, step), moved(low_face, axis, -step)


def around(value, axis):
    return [moved(value, axis, step) for step in range(1, 4)]


def swapped_cores(value):
    return lax.ppermute(value, "sx", [(i, i ^ 1) for i in range(lax.axis_size("sx"))])


def from_chips(value, chips):
    count = lax.axis_size("sx")
    far = 2 * chips - 1
    return lax.ppermute(
        value, "sx", [(i, (i + (far if i % 2 else -far)) % count) for i in range(count)]
    )


def turned_sides(low_face, high_face):
    first = lax.axis_index("sx") % 2 == 0
    inner = swapped_cores(jnp.where(first, high_face, low_face))
    return inner, from_chips(jnp.where(first, low_face, high_face), 1)


def five_chips(message):
    partner = swapped_cores(message)
    both = jnp.concatenate([message, partner], axis=0)
    near, far = from_chips(both, 1), from_chips(both, 2)
    return [message, partner, near, far, swapped_cores(jnp.concatenate([near, far], axis=0))]


def sent(value, source, target):
    return lax.ppermute(value, "tm", [(source, target)])


def shards(initial_state, start_old, end_old, coarse_old):
    begin, end, old = start_old[0], end_old[0], coarse_old[0]
    where = jnp.stack([lax.axis_index("tm"), lax.axis_index("sx") % 2]).astype(jnp.int32)

    x_low, x_high, y_low, y_high, opening = call(
        pack_body,
        [(9, 16, 128)] * 4 + [(8, 16, 128)],
        [initial_state, begin, end],
        [(4, 8, 16, 128), (4, 8, 8, 128)] + [(4, 16, 16, 128)] * 3,
        limit=56,
        far=True,
    )
    old_packed = jnp.stack(
        [jnp.concatenate([old[0], old[1]], axis=-1), jnp.concatenate([old[2], old[3]], axis=-1)]
    )
    left, right = both_sides(x_low, x_high, "sx")
    low, high = both_sides(y_low, y_high, "sy")
    comb, share, comb0 = call(
        fine_source_body,
        [(4, 16, 16, 128), (31, 16, 128), (2, 8, 8, 128)],
        [where, begin, end, left, right, low, high, old_packed, opening],
        [(4, 8, 16, 128), (4, 8, 8, 128), (2, 8, 128)],
        smem=1,
    )
    below, above = both_sides(share, share, "sy")
    across = moved(share[:23], "sy", 2)

    def coarse_down(state):
        low, high = state
        inner, outer = turned_sides(low, high)
        return call(
            coarse_down_body,
            [(4, 8, 32, 128), (12, 32, 128), (16, 128)],
            [where, inner, low, high, outer],
            [(4, 16, 32, 128), (3, 14, 32, 128), (4, 32, 128)],
            smem=1,
        )

    message, inner, outer, r0, first0 = call(
        fine_down_body,
        [(64, 128), (480, 128), (480, 128), (18, 64, 128), (10, 32, 128)],
        [where, below, share, above, across],
        [(10, 64, 128), (6, 64, 128), (4, 2, 8, 128), (6, 32, 128)],
        smem=1,
    )
    across_jump = moved(share[23:], "sy", 2)
    partner = swapped_cores(jnp.concatenate([message, inner], axis=0))
    both = jnp.concatenate([message, partner[:64]], axis=0)
    near, far, beyond = from_chips(both, 1), from_chips(both, 2), from_chips(outer, 1)
    near, far, beyond, across_jump = lax.optimization_barrier((near, far, beyond, across_jump))
    crossed = swapped_cores(jnp.concatenate([near, far], axis=0))
    got = [message, partner, near, far, crossed]
    pressure, jump0 = call(
        fine_up_body,
        [(18, 32, 128), (2, 8, 32, 128)],
        [where] + got + [partner[64:], beyond, r0, below, share, above, across_jump],
        [
            (26, 64, 128),
            (12, 64, 128),
            (40, 16, 128),
            (8, 16, 128),
            (6, 64, 128),
            (12, 64, 128),
            (10, 64, 128),
            (20, 64, 128),
            (18, 64, 128),
            (3, 8, 64, 128),
            (3, 8, 32, 128),
            (10, 32, 128),
        ],
        smem=1,
    )

    def coarse_up(body, args, scratch):
        ended, own, low, high = call(
            body,
            [(2, 8, 8, 128)] * 2 + [(2, 4, 32, 128)] * 2,
            [where] + args,
            scratch,
            smem=1,
        )
        return ended, own, [low, high]

    ended0, own1, c1 = coarse_up(
        coarse_up_first_body,
        got + [partner[64:], beyond, first0, comb0, jump0],
        [(10, 32, 128)] + UP_SCRATCH[1:] + [(12, 32, 128)],
    )
    jump1 = lax.ppermute(jump0, "tm", [(1, 0), (2, 1)])
    combined, level1, message = coarse_down(c1)
    partner = swapped_cores(message)
    both, pressure = lax.optimization_barrier(
        (jnp.concatenate([message, partner], axis=0), pressure)
    )
    near, far = from_chips(both, 1), from_chips(both, 2)
    fine_end = call(fine_end_body, (4, 16, 16, 128), [pressure, comb])
    near, far, fine_end = lax.optimization_barrier((near, far, fine_end))
    fine_before = moved(fine_end, "tm", 1)
    got = [message, partner, near, far, swapped_cores(jnp.concatenate([near, far], axis=0))]
    got, jump1 = lax.optimization_barrier((got, jump1))
    ended1, own2, c2 = coarse_up(coarse_up_middle_body, got + [combined, level1, jump1], UP_SCRATCH)

    combined, level1, message = coarse_down(c2)
    jump2 = sent(jump1, 1, 0)
    hand1 = sent(jnp.concatenate([own1, ended1], axis=0), 0, 1)
    got, hand1, jump2, fine_before = lax.optimization_barrier(
        (five_chips(message), hand1, jump2, fine_before)
    )
    ended2, own3, c3 = coarse_up(coarse_up_middle_body, got + [combined, level1, jump2], UP_SCRATCH)

    combined, level1, message = coarse_down(c3)
    hand2 = sent(jnp.concatenate([own2, ended2], axis=0), 0, 2)
    hand3 = sent(own3, 0, 3)
    got, hand2, hand3 = lax.optimization_barrier((five_chips(message), hand2, hand3))
    ended3 = call(
        coarse_up_last_body,
        (2, 8, 8, 128),
        [where] + got + [combined, level1],
        UP_SCRATCH,
        smem=1,
    )
    new_start = call(
        new_start_body,
        (4, 16, 16, 128),
        [where, fine_before, initial_state, hand1[:2] + hand2[:2] + hand3],
        [(4, 8, 16, 128), (4, 8, 8, 128), (4, 8, 16, 128)],
        smem=1,
    )
    coarse_end = call(
        coarse_end_body,
        (4, 8, 8, 64),
        [where, ended0, hand1[2:], hand2[2:], sent(ended3, 0, 3)],
        smem=1,
    )
    return (new_start[None], fine_end[None], coarse_end[None])


def solution(mesh):
    in_specs = (
        P(None, "sx", "sy", None),
        P("tm", None, "sx", "sy", None),
        P("tm", None, "sx", "sy", None),
        P("tm", None, "sx", "sy", None),
    )
    out_specs = (
        P("tm", None, "sx", "sy", None),
        P("tm", None, "sx", "sy", None),
        P("tm", None, "sx", "sy", None),
    )
    return jax.shard_map(shards, mesh=mesh, in_specs=in_specs, out_specs=out_specs, check_vma=False)
```

```python
import jax
import jax.numpy as jnp
from jax import lax
from jax.experimental import pallas as pl
from jax.experimental.pallas import tpu as pltpu
from jax.sharding import PartitionSpec as P

F32 = jnp.float32
HIGH = lax.Precision.HIGHEST


def call(body, outs, args, scratch=(), smem=0, limit=24, far=False):
    vmem = pl.BlockSpec(memory_space=pltpu.VMEM)
    scalar = pl.BlockSpec(memory_space=pltpu.SMEM)
    single = not isinstance(outs, list)
    shapes = [outs] if single else outs
    got = pl.pallas_call(
        body,
        out_shape=[jax.ShapeDtypeStruct(s, F32) for s in shapes],
        in_specs=[scalar] * smem
        + [pl.BlockSpec(memory_space=pl.ANY) if far else vmem] * (len(args) - smem),
        out_specs=[vmem] * len(shapes),
        scratch_shapes=[pltpu.VMEM(s, F32) for s in scratch]
        + ([pltpu.SemaphoreType.DMA((3, 4))] if far else []),
        compiler_params=pltpu.CompilerParams(vmem_limit_bytes=limit * 2**20),
        name=body.__name__,
    )(*args)
    return got[0] if single else got


def shifted(value, amount, axis):
    return pltpu.roll(value, amount % value.shape[axis], axis)


def nxt(value, step, axis):
    return shifted(value, -step, axis)


def prv(value, step, axis):
    return shifted(value, step, axis)


def index_along(shape, axis):
    return lax.broadcasted_iota(jnp.int32, shape, axis)


def pair_sum(value, step, axis):
    upper = (index_along(value.shape, axis) // step) % 2 == 1
    return value + jnp.where(upper, prv(value, step, axis), nxt(value, step, axis))


def ring_sum(value, step_y, step_z):
    return (
        nxt(value, step_y, 0)
        + prv(value, step_y, 0)
        + nxt(value, step_z, 1)
        + prv(value, step_z, 1)
    )


def restricted_defect(before, first, second, after, step_y, step_z):
    both = first + second
    total = both * (1.0 / 3.0) + (before + both + after + ring_sum(both, step_y, step_z)) * (1.0 / 9.0)
    return pair_sum(pair_sum(total, step_y, 0), step_z, 1) * 0.125


def smoothed(before, here, after, source, spacing_sq, step_y, step_z):
    around = before + after + ring_sum(here, step_y, step_z)
    return here * (1.0 / 3.0) + (around - spacing_sq * source) * (1.0 / 9.0)


def deep_pressure(r3, step_y, step_z):
    r4 = [
        restricted_defect(r3[2 * w], r3[2 * w + 1], r3[2 * w + 2], r3[2 * w + 3], step_y, step_z)
        for w in range(7)
    ]
    low_y, low_z = 2 * step_y, 2 * step_z
    p4 = [r * (-256.0 / 9.0) for r in r4]
    for sweep in range(2):
        inner = range(1 + sweep, 6 - sweep)
        fresh = {w: smoothed(p4[w - 1], p4[w], p4[w + 1], r4[w], 256.0, low_y, low_z) for w in inner}
        p4 = [fresh.get(w) for w in range(7)]
    e3 = {q: r3[q] * (-64.0 / 9.0) + p4[(q - 7) // 2 + 3] for q in range(5, 11)}
    return [
        smoothed(e3[q - 1], e3[q], e3[q + 1], r3[q], 64.0, step_y, step_z) for q in range(6, 10)
    ]


def advected(ref, i, comp):
    here = ref[comp, i]
    grad_x = ref[comp, i + 1] - ref[comp, i - 1]
    grad_y = nxt(here, 1, 0) - prv(here, 1, 0)
    grad_z = nxt(here, 1, 1) - prv(here, 1, 1)
    return ref[0, i] * grad_x + ref[1, i] * grad_y + ref[2, i] * grad_z


def z_pick(high):
    k = index_along((128, 128), 0)
    j = index_along((128, 128), 1)
    return jnp.where(k // 2 == j - 64 * high, 1.0, 0.0).astype(F32)


def z_spread(high):
    k = index_along((128, 128), 0)
    j = index_along((128, 128), 1)
    return jnp.where(k == j // 2 + 64 * high, 1.0, 0.0).astype(F32)


def dot(a, b):
    return lax.dot_general(a, b, (((1,), (0,)), ((), ())), precision=HIGH, preferred_element_type=F32)


def packed_pairs(half, rows):
    low, high = z_pick(0), z_pick(1)
    packed = []
    for h in range(2):
        value = dot(half[2 * h].reshape(rows, 128), low)
        if 2 * h + 1 < half.shape[0]:
            value = value + dot(half[2 * h + 1].reshape(rows, 128), high)
        packed.append(0.125 * value)
    return packed


def restricted_packed(fine, rows, half):
    for comp in range(4):
        for big in range(8):
            rows[comp, big] = fine[comp, 2 * big] + fine[comp, 2 * big + 1]
    for comp in range(4):
        for big in range(8):
            half[comp, big] = rows[comp, big, pl.ds(0, 8, 2), :] + rows[comp, big, pl.ds(1, 8, 2), :]
    return packed_pairs(half, 64)


def pack_body(
    initial_far, begin_far, end_far, x_low, x_high, y_low, y_high, opening,
    rows, half, initial, begin, end, arrived
):
    copies = [
        pltpu.make_async_copy(far.at[c], near.at[c], arrived.at[n, c])
        for n, (far, near) in enumerate(
            ((begin_far, begin), (end_far, end), (initial_far, initial))
        )
        for c in range(4)
    ]
    for copy in copies:
        copy.start()
    for copy in copies[:8]:
        copy.wait()
    for f in range(8):
        ref = begin if f < 4 else end
        x_low[f] = ref[f % 4, 0]
        x_high[f] = ref[f % 4, 15]
        for x in range(16):
            y_low[f, x : x + 1, :] = ref[f % 4, x, 0:1, :]
            y_high[f, x : x + 1, :] = ref[f % 4, x, 15:16, :]
    for copy in copies[8:]:
        copy.wait()
    packed = restricted_packed(initial, rows, half)
    for h in range(2):
        for x in range(4):
            opening[4 * h + x] = packed[h][16 * x : 16 * x + 16]
        x_low[8, 8 * h : 8 * h + 8] = packed[h][0:8]
        x_high[8, 8 * h : 8 * h + 8] = packed[h][56:64]
        for x in range(8):
            y_low[8, 8 * h + x : 8 * h + x + 1] = packed[h][8 * x : 8 * x + 1]
            y_high[8, 8 * h + x : 8 * h + x + 1] = packed[h][8 * x + 7 : 8 * x + 8]


def halves(pair):
    lane = index_along(pair.shape, 1)
    other = shifted(pair, 64, 1)
    return jnp.where(lane < 64, pair, other), jnp.where(lane < 64, other, pair)


def paired(low, high):
    return jnp.where(index_along(low.shape, 1) < 64, low, high)


def level2_pressure(r2, first, e2, step_z):
    r3 = [
        restricted_defect(
            r2[first + 2 * q + 1], r2[first + 2 * q + 2], r2[first + 2 * q + 3], r2[first + 2 * q + 4], 1, step_z
        )
        for q in range(16)
    ]
    p3 = deep_pressure(r3, 2, 2 * step_z)
    for i in range(8):
        e2[i] = r2[first + 14 + i] * (-16.0 / 9.0) + p3[i // 2]
    return [
        smoothed(e2[i], e2[i + 1], e2[i + 2], r2[first + 15 + i], 16.0, 1, step_z) for i in range(6)
    ]


def ordered(where, got, rows, base, size, blocks):
    own, partner, near, far, swapped = got
    k = where[1]
    blocks[4 + k, 0:size] = own[base : base + size]
    blocks[5 - k, 0:size] = partner[base : base + size]
    for j in range(2):
        low = rows * j + base
        turn = j * (2 * k - 1)
        blocks[3 + 3 * k + turn, 0:size] = near[low : low + size]
        blocks[1 + 7 * k + turn, 0:size] = far[low : low + size]
        blocks[6 - 3 * k - turn, 0:size] = swapped[low : low + size]
        blocks[8 - 7 * k - turn, 0:size] = swapped[2 * rows + low : 2 * rows + low + size]


def bit_lane(value, lane, step, bit):
    same = (lane // step) % 2 == bit
    return jnp.where(same, value, nxt(value, step, 1) if bit else prv(value, step, 1))


def fine_source_body(
    where, begin, end, left, right, low, high, old, opening, comb, out, comb0, rows, half, rim
):
    row = index_along((16, 128), 0)
    first, last = row == 0, row == 15

    def at(f, x):
        if x < 0:
            return left[f]
        if x > 15:
            return right[f]
        return (begin if f < 4 else end)[f % 4, x]

    def carried(f, x):
        base = f - f % 4
        here = at(f, x)
        grad_x = at(f, x + 1) - at(f, x - 1)
        above = jnp.where(last, high[f, x : x + 1, :], nxt(here, 1, 0))
        below = jnp.where(first, low[f, x : x + 1, :], prv(here, 1, 0))
        grad_z = nxt(here, 1, 1) - prv(here, 1, 1)
        return at(base, x) * grad_x + at(base + 1, x) * (above - below) + at(base + 2, x) * grad_z

    for x in range(16):
        for c in range(4):
            total = begin[c, x] - 0.125 * (carried(c, x) + carried(c + 4, x))
            if c == 2:
                total = total + 0.25 * (begin[3, x] + end[3, x])
            comb[c, x] = total
    out[0] = 0.5 * comb[0, 0]
    out[17] = -0.5 * comb[0, 15]
    for x in range(16):
        v = comb[1, x]
        w = comb[2, x]
        div = jnp.where(last, 0.0, nxt(v, 1, 0)) - jnp.where(first, 0.0, prv(v, 1, 0))
        div = div + nxt(w, 1, 1) - prv(w, 1, 1)
        if x < 15:
            div = div + comb[0, x + 1]
        if x > 0:
            div = div - comb[0, x - 1]
        out[x + 1] = 0.5 * div
        out[18, x : x + 1, :] = 0.5 * v[0:1]
        out[19, x : x + 1, :] = -0.5 * v[15:16]
    coarse_source(opening, left, right, low, high, comb0, out, rim)
    packed = restricted_packed(comb, rows, half)
    for h in range(2):
        for x in range(4):
            for n in range(2):
                part = packed[h][16 * x + 8 * n : 16 * x + 8 * n + 8] - old[h, 2 * x + n]
                part = part + jnp.where(where[0] == 0, comb0[h, 2 * x + n], 0.0)
                out[23 + 4 * h + x, 8 * n : 8 * n + 8] = part


def coarse_source(opening, left, right, low, high, comb0, out, rim):
    row = index_along((8, 128), 0)

    def inside(x):
        rows = 8 * (x % 2)
        return [
            *halves(opening[x // 2, rows : rows + 8]),
            *halves(opening[4 + x // 2, rows : rows + 8]),
        ]

    def outside(ref):
        return [*halves(ref[8, 0:8]), *halves(ref[8, 8:16])]

    plane = {x: inside(x) for x in range(8)}
    plane[-1], plane[8] = outside(left), outside(right)
    under, over = outside(low), outside(high)
    comb = []
    for x in range(8):
        u, v, w, b = plane[x]
        fresh = []
        for c in range(4):
            here = plane[x][c]
            above = jnp.where(row == 7, over[c][x : x + 1], nxt(here, 1, 0))
            below = jnp.where(row == 0, under[c][x : x + 1], prv(here, 1, 0))
            moving = u * (plane[x + 1][c] - plane[x - 1][c]) + v * (above - below)
            moving = moving + w * (nxt(here, 1, 1) - prv(here, 1, 1))
            fresh.append(here - 0.125 * moving + (0.5 * b if c == 2 else 0.0))
        comb.append(fresh)
        comb0[0, x] = paired(fresh[0], fresh[1])
        comb0[1, x] = paired(fresh[2], fresh[3])
    source = [0.25 * comb[0][0]]
    for x in range(8):
        u, v, w, b = comb[x]
        div = jnp.where(row == 7, 0.0, nxt(v, 1, 0)) - jnp.where(row == 0, 0.0, prv(v, 1, 0))
        div = div + nxt(w, 1, 1) - prv(w, 1, 1)
        if x < 7:
            div = div + comb[x + 1][0]
        if x > 0:
            div = div - comb[x - 1][0]
        source.append(0.25 * div)
        rim[0, x : x + 1, :] = 0.25 * v[0:1]
        rim[1, x : x + 1, :] = -0.25 * v[7:8]
    source.append(-0.25 * comb[7][0])
    source += [rim[0], rim[1]]
    for i in range(6):
        out[20 + i // 2, 8 * (i % 2) : 8 * (i % 2) + 8] = paired(source[2 * i], source[2 * i + 1])


def fine_down_body(
    where, below, own, above, across,
    message, inner, outer, r0, coarse_r1, r1, r2, rim, coarse_r2
):
    blocks = (below, own, above, across)
    for b, ref in enumerate(blocks):
        r0[:, 16 * b : 16 * b + 16] = ref[0:18]
    for b, ref in enumerate(blocks):
        for i in range(6):
            pair = halves(ref[20 + i // 2, 8 * (i % 2) : 8 * (i % 2) + 8])
            for n in range(2):
                if i < 5:
                    coarse_r1[2 * i + n, 8 * b : 8 * b + 8] = pair[n]
                else:
                    rim[b, n] = pair[n]
    for b in range(4):
        for x in range(8):
            coarse_r1[x + 1, 8 * b + 7 : 8 * b + 8] += rim[(b + 1) % 4, 0, x : x + 1, :]
            coarse_r1[x + 1, 8 * b : 8 * b + 1] += rim[(b + 3) % 4, 1, x : x + 1, :]
    nothing = jnp.zeros((32, 128), F32)

    def at(x):
        return coarse_r1[x + 1] if -1 <= x < 9 else nothing

    for x in range(-1, 5):
        coarse_r2[x + 1] = restricted_defect(at(2 * x - 1), at(2 * x), at(2 * x + 1), at(2 * x + 2), 1, 1)
    for b in range(4):
        upper, lower = blocks[(b + 1) % 4], blocks[(b + 3) % 4]
        for x in range(16):
            r0[x + 1, 16 * b + 15 : 16 * b + 16] += upper[18, x : x + 1, :]
            r0[x + 1, 16 * b : 16 * b + 1] += lower[19, x : x + 1, :]
    zero = jnp.zeros((64, 128), F32)

    def at0(x):
        return r0[x + 1] if -1 <= x < 17 else zero

    def at1(x):
        return r1[x + 1] if -1 <= x < 9 else zero

    for x in range(-1, 9):
        r1[x + 1] = restricted_defect(at0(2 * x - 1), at0(2 * x), at0(2 * x + 1), at0(2 * x + 2), 1, 1)
    for x in range(-1, 5):
        r2[x + 1] = restricted_defect(at1(2 * x - 1), at1(2 * x), at1(2 * x + 1), at1(2 * x + 2), 2, 2)
    lane = index_along((16, 128), 1)
    part = [r2[i, pl.ds(0, 16, 4), :] for i in range(6)]
    odd = lane % 2 == 1
    first = jnp.where(
        lane % 4 < 2, jnp.where(odd, part[1], part[0]), jnp.where(odd, part[3], part[2])
    )
    second = jnp.where(odd, part[5], part[4])
    message[0:16] = first
    message[16:32] = second
    part = [coarse_r2[i, pl.ds(0, 16, 2), :] for i in range(6)]
    message[32:48] = paired(jnp.where(odd, part[1], part[0]), jnp.where(odd, part[3], part[2]))
    message[48:64] = jnp.where(odd, part[5], part[4])
    k = where[1]
    for i in range(3):
        inner[384 + 32 * i : 416 + 32 * i] = coarse_r1[7 - 7 * k + i]
        outer[384 + 32 * i : 416 + 32 * i] = coarse_r1[7 * k + i]
    for i in range(6):
        inner[64 * i : 64 * i + 64] = r0[12 - 12 * k + i]
        outer[64 * i : 64 * i + 64] = r0[12 * k + i]


def sum_parts(parts, r2):
    for j in range(10):
        for n in range(4):
            value = parts[j][n + 1]
            if n == 0 and j > 0:
                value = value + parts[j - 1][5]
            if n == 3 and j < 9:
                value = value + parts[j + 1][0]
            r2[4 * j + n] = value


def fine_up_body(
    where, own, partner, near, far, swapped, face_in, face_out, mine, below, own_share, above, across_jump, pressure, jump,
    r0, r1, r2, e2, p2, e1, p1, e0, p0, rows, half, blocks
):
    k = where[1]
    ordered(where, (own, partner, near, far, swapped), 64, 0, 32, blocks)
    r0[5:21] = mine[1:17]
    for i in range(6):
        inside = face_in[64 * i : 64 * i + 64]
        outside = face_out[64 * i : 64 * i + 64]
        left = jnp.where(k == 0, outside, inside)
        right = jnp.where(k == 0, inside, outside)
        if i < 5:
            r0[i] = left
        else:
            r0[5] += left
        if i > 0:
            r0[20 + i] = right
        else:
            r0[20] += right
    r0[4] += mine[0]
    r0[21] += mine[17]
    lane = index_along((16, 128), 1)
    parts = []
    for j in range(10):
        first, second = blocks[j, 0:16], blocks[j, 16:32]
        even, odd = bit_lane(first, lane, 2, 0), bit_lane(first, lane, 2, 1)
        parts.append(
            [
                bit_lane(even, lane, 1, 0),
                bit_lane(even, lane, 1, 1),
                bit_lane(odd, lane, 1, 0),
                bit_lane(odd, lane, 1, 1),
                bit_lane(second, lane, 1, 0),
                bit_lane(second, lane, 1, 1),
            ]
        )
    sum_parts(parts, r2)
    for i, value in enumerate(level2_pressure(r2, 4 * k, e2, 4)):
        for y2 in range(16):
            p2[i, 4 * y2 : 4 * y2 + 4, :] = jnp.broadcast_to(value[y2 : y2 + 1], (4, 128))
    for k in range(12):
        a = 2 * k + 1
        r1[k] = restricted_defect(r0[a - 1], r0[a], r0[a + 1], r0[a + 2], 1, 1)
        e1[k] = r1[k] * (-4.0 / 9.0) + p2[k // 2]
    for k in range(10):
        p1[k] = smoothed(e1[k], e1[k + 1], e1[k + 2], r1[k + 1], 4.0, 2, 2)
    for j in range(20):
        e0[j] = r0[j + 3] * (-1.0 / 9.0) + p1[j // 2]
    for j in range(18):
        p0[j] = smoothed(e0[j], e0[j + 1], e0[j + 2], r0[j + 4], 1.0, 1, 1)
    for big in range(8):
        a = 2 * big + 1
        pair = p0[a] + p0[a + 1]
        rows[0, big] = p0[a + 1] + p0[a + 2] - p0[a - 1] - p0[a]
        rows[1, big] = nxt(pair, 1, 0) - prv(pair, 1, 0)
        rows[2, big] = nxt(pair, 1, 1) - prv(pair, 1, 1)
    for c in range(3):
        for big in range(8):
            half[c, big] = rows[c, big, pl.ds(0, 32, 2), :] + rows[c, big, pl.ds(1, 32, 2), :]
    packed = packed_pairs(half, 256)
    for h in range(2):
        slope = 0.5 * packed[h].reshape(8, 32, 128)
        for b, (ref, first) in enumerate(((below, 23), (own_share, 23), (above, 23), (across_jump, 0))):
            for x in range(8):
                jump[h, x, 8 * b : 8 * b + 8] = (
                    ref[first + 4 * h + x // 2, 8 * (x % 2) : 8 * (x % 2) + 8]
                    - slope[x, 8 * b : 8 * b + 8]
                )
    pressure[...] = p0[:, 8:40]


def fine_end_body(pressure, comb, fine):
    for x in range(16):
        here = pressure[x + 1]
        mid = here[8:24]
        fine[0, x] = comb[0, x] - 0.5 * (pressure[x + 2, 8:24] - pressure[x, 8:24])
        fine[1, x] = comb[1, x] - 0.5 * (nxt(here, 1, 0) - prv(here, 1, 0))[8:24]
        fine[2, x] = comb[2, x] - 0.5 * (nxt(mid, 1, 1) - prv(mid, 1, 1))
        fine[3, x] = comb[3, x]


def coarse_down_body(where, inner, low, high, outer, comb_out, r1, message, state, comb, r2):
    lane = index_along((32, 128), 1)
    k = where[1]
    for side, ref in enumerate((outer, low, high, inner)):
        for x in range(4):
            for h in range(2):
                pair = ref[h, x]
                if side in (0, 3):
                    pair = jnp.where(k == 0, pair, (inner if side == 0 else outer)[h, x])
                other = shifted(pair, 64, 1)
                state[2 * h, 4 * side + x] = jnp.where(lane < 64, pair, other)
                state[2 * h + 1, 4 * side + x] = jnp.where(lane < 64, other, pair)
    message[...] = coarse_down_core(comb_out, r1, state, comb, r2)


def coarse_down_core(comb_out, r1, state, comb, r2):
    for i in range(1, 15):
        for c in range(3):
            total = state[c, i] - 0.125 * advected(state, i, c)
            if c == 2:
                total = total + 0.5 * state[3, i]
            comb[c, i - 1] = total
            if 4 <= i < 12:
                comb_out[c, i - 4] = total
    for x in range(8):
        comb_out[3, x] = state[3, x + 4] - 0.125 * advected(state, x + 4, 3)
    for k in range(12):
        v = comb[1, k + 1]
        w = comb[2, k + 1]
        div = comb[0, k + 2] - comb[0, k] + nxt(v, 1, 0) - prv(v, 1, 0) + nxt(w, 1, 1) - prv(w, 1, 1)
        r1[k] = 0.25 * div
    for m in range(4):
        a = 2 * m + 2
        r2[m] = restricted_defect(r1[a - 1], r1[a], r1[a + 1], r1[a + 2], 1, 1)
    part = [r2[m, pl.ds(0, 16, 2), :] for m in range(4)]
    lane = index_along((16, 128), 1)
    odd = lane % 2 == 1
    return jnp.where(
        lane < 64, jnp.where(odd, part[1], part[0]), jnp.where(odd, part[3], part[2])
    )


def coarse_up_core(where, got, comb, r1, blocks, r2, e2, p2, e1, p1, emit):
    ordered(where, got, 16, 0, 16, blocks)
    lane = index_along((16, 128), 1)
    for j in range(10):
        for m, pair in enumerate(halves(blocks[j])):
            r2[4 * j + 2 * m] = bit_lane(pair, lane, 1, 0)
            r2[4 * j + 2 * m + 1] = bit_lane(pair, lane, 1, 1)
    level1_pressure(where, r1, r2, e2, p2, e1, p1)
    for x in range(8):
        u, v, w = slopes(p1, x)
        emit(0, x, paired(comb[0, x] - u, comb[1, x] - v))
        emit(1, x, paired(comb[2, x] - w, comb[3, x]))


def level1_pressure(where, r1, r2, e2, p2, e1, p1):
    for i, value in enumerate(level2_pressure(r2, 4 * where[1], e2, 2)):
        p2[i, pl.ds(0, 16, 2), :] = value
        p2[i, pl.ds(1, 16, 2), :] = value
    for k in range(12):
        e1[k] = r1[k] * (-4.0 / 9.0) + p2[k // 2]
    for k in range(10):
        p1[k] = smoothed(e1[k], e1[k + 1], e1[k + 2], r1[k + 1], 4.0, 1, 1)


def slopes(p1, x):
    here = p1[x + 1]
    return (
        0.25 * (p1[x + 2] - p1[x]),
        0.25 * (nxt(here, 1, 0) - prv(here, 1, 0)),
        0.25 * (nxt(here, 1, 1) - prv(here, 1, 1)),
    )


UP_SCRATCH = [(10, 16, 128), (40, 16, 128), (8, 16, 128), (6, 32, 128), (12, 32, 128), (10, 32, 128)]


def coarse_up_first_body(
    where, own, partner, near, far, swapped, face_in, face_out, mine, comb0, jump,
    ended, after, low, high, blocks, r2, e2, p2, e1, p1, r1
):
    k = where[1]
    ordered(where, (own, partner, near, far, swapped), 64, 32, 32, blocks)
    lane = index_along((16, 128), 1)
    parts = []
    for j in range(10):
        second = blocks[j, 16:32]
        shares = []
        for pair in halves(blocks[j, 0:16]):
            shares += [bit_lane(pair, lane, 1, 0), bit_lane(pair, lane, 1, 1)]
        parts.append(shares + [bit_lane(second, lane, 1, 0), bit_lane(second, lane, 1, 1)])
    sum_parts(parts, r2)
    r1[2:10] = mine[1:9]
    for i in range(3):
        inside = face_in[384 + 32 * i : 416 + 32 * i]
        outside = face_out[384 + 32 * i : 416 + 32 * i]
        left = jnp.where(k == 0, outside, inside)
        right = jnp.where(k == 0, inside, outside)
        if i < 2:
            r1[i] = left
        else:
            r1[2] += left
        if i > 0:
            r1[9 + i] = right
        else:
            r1[9] += right
    r1[1] += mine[0]
    r1[10] += mine[9]
    level1_pressure(where, r1, r2, e2, p2, e1, p1)
    for x in range(8):
        u, v, w = slopes(p1, x)
        for h, change in enumerate((paired(u, v), paired(w, jnp.zeros_like(w)))):
            value = jump[h, x] - change
            ref = low if x < 4 else high
            ref[h, x % 4] = value
            after[h, x] = value[8:16]
            ended[h, x] = comb0[h, x] - change[8:16]


def coarse_up_middle_body(where, a, b, c, d, e, comb, r1, jump, ended, own, low, high, *scratch):
    def emit(h, x, value):
        after = value + jump[h, x]
        ref = low if x < 4 else high
        ref[h, x % 4] = after
        ended[h, x] = value[8:16]
        own[h, x] = after[8:16]

    coarse_up_core(where, (a, b, c, d, e), comb, r1, *scratch, emit)


def coarse_up_last_body(where, a, b, c, d, e, comb, r1, ended, *scratch):
    def emit(h, x, value):
        ended[h, x] = value[8:16]

    coarse_up_core(where, (a, b, c, d, e), comb, r1, *scratch, emit)


def new_start_body(where, fine, initial, state, out, rows, half, tall):
    t = where[0]

    @pl.when(t == 0)
    def _():
        out[...] = initial[...]

    @pl.when(t > 0)
    def _():
        packed = restricted_packed(fine, rows, half)
        for h in range(2):
            change = state[h].reshape(64, 128) - packed[h]
            for side in range(2):
                comp = 2 * h + side
                wide = dot(change, z_spread(side)).reshape(8, 8, 128)
                for x in range(8):
                    tall[comp, x, pl.ds(0, 8, 2), :] = wide[x]
                    tall[comp, x, pl.ds(1, 8, 2), :] = wide[x]
        for comp in range(4):
            for x in range(16):
                out[comp, x] = fine[comp, x] + tall[comp, x // 2]


def coarse_end_body(where, e0, e1, e2, e3, out):
    t = where[0]
    for h in range(2):
        low = jnp.where(t == 0, e0[h], e1[h])
        high = jnp.where(t == 2, e2[h], e3[h])
        value = jnp.where(t < 2, low, high)
        out[2 * h] = value[:, :, :64]
        out[2 * h + 1] = shifted(value, 64, 2)[:, :, :64]


def moved(value, axis, step):
    count = lax.axis_size(axis)
    return lax.ppermute(value, axis, [(i, (i + step) % count) for i in range(count)])


def both_sides(low_face, high_face, axis, step=1):
    return moved(high_face, axis, step), moved(low_face, axis, -step)


def around(value, axis):
    return [moved(value, axis, step) for step in range(1, 4)]


def swapped_cores(value):
    return lax.ppermute(value, "sx", [(i, i ^ 1) for i in range(lax.axis_size("sx"))])


def from_chips(value, chips):
    count = lax.axis_size("sx")
    far = 2 * chips - 1
    return lax.ppermute(
        value, "sx", [(i, (i + (far if i % 2 else -far)) % count) for i in range(count)]
    )


def turned_sides(low_face, high_face):
    first = lax.axis_index("sx") % 2 == 0
    inner = swapped_cores(jnp.where(first, high_face, low_face))
    return inner, from_chips(jnp.where(first, low_face, high_face), 1)


def five_chips(message):
    partner = swapped_cores(message)
    both = jnp.concatenate([message, partner], axis=0)
    near, far = from_chips(both, 1), from_chips(both, 2)
    return [message, partner, near, far, swapped_cores(jnp.concatenate([near, far], axis=0))]


def sent(value, source, target):
    return lax.ppermute(value, "tm", [(source, target)])


def shards(initial_state, start_old, end_old, coarse_old):
    begin, end, old = start_old[0], end_old[0], coarse_old[0]
    where = jnp.stack([lax.axis_index("tm"), lax.axis_index("sx") % 2]).astype(jnp.int32)

    x_low, x_high, y_low, y_high, opening = call(
        pack_body,
        [(9, 16, 128)] * 4 + [(8, 16, 128)],
        [initial_state, begin, end],
        [(4, 8, 16, 128), (4, 8, 8, 128)] + [(4, 16, 16, 128)] * 3,
        limit=56,
        far=True,
    )
    old_packed = jnp.stack(
        [jnp.concatenate([old[0], old[1]], axis=-1), jnp.concatenate([old[2], old[3]], axis=-1)]
    )
    left, right = both_sides(x_low, x_high, "sx")
    low, high = both_sides(y_low, y_high, "sy")
    comb, share, comb0 = call(
        fine_source_body,
        [(4, 16, 16, 128), (31, 16, 128), (2, 8, 8, 128)],
        [where, begin, end, left, right, low, high, old_packed, opening],
        [(4, 8, 16, 128), (4, 8, 8, 128), (2, 8, 128)],
        smem=1,
    )
    below, above = both_sides(share, share, "sy")
    across = moved(share[:23], "sy", 2)

    def coarse_down(state):
        low, high = state
        inner, outer = turned_sides(low, high)
        return call(
            coarse_down_body,
            [(4, 8, 32, 128), (12, 32, 128), (16, 128)],
            [where, inner, low, high, outer],
            [(4, 16, 32, 128), (3, 14, 32, 128), (4, 32, 128)],
            smem=1,
        )

    message, inner, outer, r0, first0 = call(
        fine_down_body,
        [(64, 128), (480, 128), (480, 128), (18, 64, 128), (10, 32, 128)],
        [where, below, share, above, across],
        [(10, 64, 128), (6, 64, 128), (4, 2, 8, 128), (6, 32, 128)],
        smem=1,
    )
    across_jump = moved(share[23:], "sy", 2)
    partner = swapped_cores(jnp.concatenate([message, inner], axis=0))
    both = jnp.concatenate([message, partner[:64]], axis=0)
    near, far, beyond = from_chips(both, 1), from_chips(both, 2), from_chips(outer, 1)
    near, far, beyond, across_jump = lax.optimization_barrier((near, far, beyond, across_jump))
    crossed = swapped_cores(jnp.concatenate([near, far], axis=0))
    got = [message, partner, near, far, crossed]
    pressure, jump0 = call(
        fine_up_body,
        [(18, 32, 128), (2, 8, 32, 128)],
        [where] + got + [partner[64:], beyond, r0, below, share, above, across_jump],
        [
            (26, 64, 128),
            (12, 64, 128),
            (40, 16, 128),
            (8, 16, 128),
            (6, 64, 128),
            (12, 64, 128),
            (10, 64, 128),
            (20, 64, 128),
            (18, 64, 128),
            (3, 8, 64, 128),
            (3, 8, 32, 128),
            (10, 32, 128),
        ],
        smem=1,
    )

    def coarse_up(body, args, scratch):
        ended, own, low, high = call(
            body,
            [(2, 8, 8, 128)] * 2 + [(2, 4, 32, 128)] * 2,
            [where] + args,
            scratch,
            smem=1,
        )
        return ended, own, [low, high]

    ended0, own1, c1 = coarse_up(
        coarse_up_first_body,
        got + [partner[64:], beyond, first0, comb0, jump0],
        [(10, 32, 128)] + UP_SCRATCH[1:] + [(12, 32, 128)],
    )
    jump1 = lax.ppermute(jump0, "tm", [(1, 0), (2, 1)])
    combined, level1, message = coarse_down(c1)
    partner = swapped_cores(message)
    both, pressure = lax.optimization_barrier(
        (jnp.concatenate([message, partner], axis=0), pressure)
    )
    near, far = from_chips(both, 1), from_chips(both, 2)
    fine_end = call(fine_end_body, (4, 16, 16, 128), [pressure, comb])
    near, far, fine_end = lax.optimization_barrier((near, far, fine_end))
    fine_before = moved(fine_end, "tm", 1)
    got = [message, partner, near, far, swapped_cores(jnp.concatenate([near, far], axis=0))]
    got, jump1 = lax.optimization_barrier((got, jump1))
    ended1, own2, c2 = coarse_up(coarse_up_middle_body, got + [combined, level1, jump1], UP_SCRATCH)

    combined, level1, message = coarse_down(c2)
    jump2 = sent(jump1, 1, 0)
    hand1 = sent(jnp.concatenate([own1, ended1], axis=0), 0, 1)
    got, jump2, fine_before = lax.optimization_barrier((five_chips(message), jump2, fine_before))
    ended2, own3, c3 = coarse_up(coarse_up_middle_body, got + [combined, level1, jump2], UP_SCRATCH)

    combined, level1, message = coarse_down(c3)
    hand2 = sent(jnp.concatenate([own2, ended2], axis=0), 0, 2)
    hand3 = sent(own3, 0, 3)
    got, hand1, hand2, hand3 = lax.optimization_barrier(
        (five_chips(message), hand1, hand2, hand3)
    )
    ended3 = call(
        coarse_up_last_body,
        (2, 8, 8, 128),
        [where] + got + [combined, level1],
        UP_SCRATCH,
        smem=1,
    )
    new_start = call(
        new_start_body,
        (4, 16, 16, 128),
        [where, fine_before, initial_state, hand1[:2] + hand2[:2] + hand3],
        [(4, 8, 16, 128), (4, 8, 8, 128), (4, 8, 16, 128)],
        smem=1,
    )
    coarse_end = call(
        coarse_end_body,
        (4, 8, 8, 64),
        [where, ended0, hand1[2:], hand2[2:], sent(ended3, 0, 3)],
        smem=1,
    )
    return (new_start[None], fine_end[None], coarse_end[None])


def solution(mesh):
    in_specs = (
        P(None, "sx", "sy", None),
        P("tm", None, "sx", "sy", None),
        P("tm", None, "sx", "sy", None),
        P("tm", None, "sx", "sy", None),
    )
    out_specs = (
        P("tm", None, "sx", "sy", None),
        P("tm", None, "sx", "sy", None),
        P("tm", None, "sx", "sy", None),
    )
    return jax.shard_map(shards, mesh=mesh, in_specs=in_specs, out_specs=out_specs, check_vma=False)
```
